32 devices in a mesh: segment: 4 (over x, core), expert: 4 (over z), fsdp: 2 (over y).
Axes of the slice: x: 2, y: 2, z: 4, core: 2. Of those that a mesh axis runs over, the one named last changes fastest.
Arguments:
- acts: bfloat16 [4, 2, 128, 1024], P('segment', None, ('expert', 'fsdp')), may hold values from -6 to 6
- out_grad: bfloat16 [2, 128, 1024], P(None, ('expert', 'fsdp')), may hold values from -6 to 6
- expert_ids: int32 [4, 2, 128, 2], P('segment', None, ('expert', 'fsdp')), may hold values from 0 to 3, all different within a row; in each aligned block of 16 rows (0 to 15, 16 to 31, ..., all dimensions but the last counted through in order) at most 10 rows name the same one
- gates: bfloat16 [4, 2, 128, 2], P('segment', None, ('expert', 'fsdp')), may hold values from 0.19921875 to 1
- w_gate: bfloat16 [4, 4, 1024, 2048], P('segment', 'expert', None, 'fsdp'), may hold values from -0.1875 to 0.1875
- w_up: bfloat16 [4, 4, 1024, 2048], P('segment', 'expert', None, 'fsdp'), may hold values from -0.1875 to 0.1875
- w_down: bfloat16 [4, 4, 2048, 1024], P('segment', 'expert', 'fsdp'), may hold values from -0.125 to 0.125
Outputs:
- act_grad: bfloat16 [4, 2, 128, 1024], P('segment', None, ('expert', 'fsdp'))
- gate_grad: float32 [4, 2, 128, 2], P('segment', None, ('expert', 'fsdp'))
- grad_w_gate: bfloat16 [4, 4, 1024, 2048], P('segment', 'expert', None, 'fsdp')
- grad_w_up: bfloat16 [4, 4, 1024, 2048], P('segment', 'expert', None, 'fsdp')
- grad_w_down: bfloat16 [4, 4, 2048, 1024], P('segment', 'expert', 'fsdp')
The draws below stay inside these ranges and needn't reach their ends.
Inputs may be any that keep to these rules, and one draw needn't show every extreme that they name: `expert_ids`: each row names 2 different experts. Within the tokens of one device for one layer and micro-batch (aligned blocks of 16 rows) no expert is named by more than 10 tokens, and in some such block an expert is named by exactly 10.
All inputs are finite; a program needn't handle non-finite values.
Results may differ from the reference program's by a relative error of at most 0.035.
Values may be sent and summed in bfloat16 or wider, within the bound.
A program may use at most 64 MiB of HBM per device.

```python
import math
import jax
import jax.numpy as jnp
import numpy as np
from jax import lax

D = 1024
HID = 2048
TOP = 2
MB = 2
TOK_DEV = 16
SEGMENTS = 4
EXPERTS = 4
TOKENS = 128
CAP = 10
N_EXPERT = 4
N_FSDP = 2


def block_levels(own_key, extent, cuts, least, largest):
    loudness = 1.0
    for dim, blocks in cuts:
        steps = jax.random.uniform(jax.random.fold_in(jax.random.fold_in(own_key, 6), dim), (blocks,), jnp.float32, least / len(cuts), largest / len(cuts))
        loudness = loudness * jnp.repeat(jnp.exp(steps), extent[dim] // blocks).reshape((-1,) + (1,) * (len(extent) - 1 - dim))
    return loudness


def shared_out(own_key, own, number, rows, amount, top, bound, skew):
    order = jax.random.permutation(own_key, amount)
    heavy_load, usual = shares(amount, rows * top, bound, skew, True), shares(amount, rows * top, bound, skew, False)
    places = jnp.arange(amount)

    def named(lengths, turn):
        used = int((lengths > 0).sum())
        fixed = max(1, used // 4)
        moved = fixed + (places - fixed + turn * (used - fixed)) % max(1, amount - fixed)
        return jnp.zeros((amount,), jnp.int32).at[order[jnp.where(places < fixed, places, moved)]].set(jnp.asarray(lengths, jnp.int32))

    lengths = jnp.where(number % 4 == 0, named(heavy_load, number // 4), named(usual, number - number // 4 - 1))
    mixed = jax.random.permutation(jax.random.fold_in(own, 3), amount)
    giver, taker = mixed[0:amount // 2 * 2:2], mixed[1:amount // 2 * 2:2]
    margin = jnp.minimum(lengths[giver] - 1, bound - lengths[taker]) // 2
    margin = jnp.where((giver == order[0]) | (taker == order[0]) | (lengths[taker] == 0), 0, jnp.maximum(margin, 0))
    moved = jax.random.randint(jax.random.fold_in(own, 4), (amount // 2,), 0, 1 << 20) % (margin + 1)
    lengths = lengths.at[giver].add(-moved).at[taker].add(moved)
    members = jnp.searchsorted(jnp.cumsum(lengths), jnp.arange(rows * top), side="right").astype(jnp.int32)
    table = members.reshape(top, rows).T
    table = table[jax.random.permutation(jax.random.fold_in(own, 1), rows)]
    turn = jax.random.randint(jax.random.fold_in(own, 2), (rows, 1), 0, top)
    return jnp.take_along_axis(table, (jnp.arange(top)[None, :] + turn) % top, axis=1)


def shares(number_of, total, bound, slope, full):
    weights = [(1 << 20) // math.isqrt(rank ** slope) + 1 for rank in range(1, number_of + 1)]
    largest = bound if full else min(bound, max(-(-total // number_of), total * weights[0] // sum(weights)))
    least = 1 if total - largest >= number_of - 1 else 0
    given, rest = [largest] + [least] * (number_of - 1), total - largest - least * (number_of - 1)
    while rest > 0:
        free = [i for i in range(1, number_of) if given[i] < largest] or [i for i in range(1, number_of) if given[i] < bound]
        mass, left = sum([weights[i] for i in free]), rest
        for i in free:
            addition = min(bound - given[i], max(1, left * weights[i] // mass), rest)
            given[i] = given[i] + addition
            rest = rest - addition
    return np.array(given)


def gaussian(rng, dims, width, reach, cuts=(), held_as=jnp.bfloat16):
    entries = jax.random.normal(rng, dims, jnp.float32) * width
    if len(cuts) > 0:
        entries = block_levels(rng, dims, cuts, -0.22, 0.18) * entries
    return jnp.clip(entries, min=-reach, max=reach).astype(held_as)


def setup_inputs(seed: int = 0) -> dict:
    key_of = jax.random.split(jax.random.key(seed), 8)
    acts = gaussian(key_of[0], (SEGMENTS, MB, TOKENS, D), 1.0, 6.0, ((0, 4), (2, 8)))
    out_grad = gaussian(key_of[1], (MB, TOKENS, D), 1.0, 6.0, ((1, 8),))
    expert_ids_keys = jax.random.split(jax.random.fold_in(key_of[2], 1), SEGMENTS * MB * TOKENS // TOK_DEV)
    expert_ids_turns = jax.random.permutation(jax.random.fold_in(key_of[2], 3), SEGMENTS * MB * TOKENS // TOK_DEV)
    expert_ids = jax.vmap(lambda own, number: shared_out(jax.random.fold_in(key_of[2], 2), own, number, TOK_DEV, EXPERTS, TOP, CAP, 2))(expert_ids_keys, expert_ids_turns).reshape((SEGMENTS, MB, TOKENS, TOP))
    gates = jnp.clip(0.19921875 + 0.80078125 * jax.random.uniform(key_of[3], (SEGMENTS, MB, TOKENS, TOP), jnp.float32) ** block_levels(key_of[3], (SEGMENTS, MB, TOKENS, TOP), ((0, 4), (2, 8)), -0.2, 0.2), 0.19921875, 1.0).astype(jnp.bfloat16)
    w_gate = gaussian(key_of[4], (SEGMENTS, EXPERTS, D, HID), D ** -0.5, 0.1875, ((0, 4), (1, 4), (3, 2)))
    w_up = gaussian(key_of[5], (SEGMENTS, EXPERTS, D, HID), D ** -0.5, 0.1875, ((0, 4), (1, 4), (3, 2)))
    w_down = gaussian(key_of[6], (SEGMENTS, EXPERTS, HID, D), HID ** -0.5, 0.125, ((0, 4), (1, 4), (2, 2)))
    return {"acts": acts, "out_grad": out_grad, "expert_ids": expert_ids, "gates": gates, "w_gate": w_gate, "w_up": w_up, "w_down": w_down}


def silu_parts(pre_gate):
    sigmoid = jax.nn.sigmoid(pre_gate)
    return pre_gate * sigmoid, sigmoid * (1.0 + pre_gate * (1.0 - sigmoid))


def expert_backward(packed):
    token_rows, grad_rows, gate_rows, w_first, w_third, w_second = packed
    pre_gate = jnp.dot(token_rows, w_first, preferred_element_type=jnp.float32)
    pre_up = jnp.dot(token_rows, w_third, preferred_element_type=jnp.float32)
    activated, slope_term = silu_parts(pre_gate)
    hidden = activated * pre_up
    back_hidden = jnp.dot(grad_rows, w_second.T, preferred_element_type=jnp.float32)
    gate_col = gate_rows.astype(jnp.float32)[:, None]
    scaled = back_hidden * gate_col
    grad_gate_pre = (scaled * pre_up * slope_term).astype(jnp.bfloat16)
    grad_up_pre = (scaled * activated).astype(jnp.bfloat16)
    hidden_gated = (hidden * gate_col).astype(jnp.bfloat16)
    grad_first = jnp.dot(token_rows.T, grad_gate_pre, preferred_element_type=jnp.float32)
    grad_third = jnp.dot(token_rows.T, grad_up_pre, preferred_element_type=jnp.float32)
    grad_second = jnp.dot(hidden_gated.T, grad_rows, preferred_element_type=jnp.float32)
    row_count = token_rows.shape[0]
    block_width = HID // N_FSDP
    part_rows = jnp.einsum('rch,dch->rcd', grad_gate_pre.astype(jnp.float32).reshape(row_count, N_FSDP, block_width), w_first.astype(jnp.float32).reshape(D, N_FSDP, block_width))
    part_rows = part_rows + jnp.einsum('rch,dch->rcd', grad_up_pre.astype(jnp.float32).reshape(row_count, N_FSDP, block_width), w_third.astype(jnp.float32).reshape(D, N_FSDP, block_width))
    part_rows = lax.optimization_barrier(part_rows.astype(jnp.bfloat16))
    row_grad = jnp.sum(part_rows.astype(jnp.float32), axis=1).astype(jnp.bfloat16)
    part_gates = jnp.sum((hidden * back_hidden).reshape(row_count, N_FSDP, block_width), axis=2)
    part_gates = lax.optimization_barrier(part_gates.astype(jnp.bfloat16))
    gate_sum = jnp.sum(part_gates.astype(jnp.float32), axis=1).astype(jnp.bfloat16)
    return row_grad, gate_sum, grad_first, grad_third, grad_second


def layer_backward(acts_in, grad_in, ids_in, gates_in, w_first_all, w_third_all, w_second_all):
    sources = N_EXPERT * N_FSDP
    ids_block = ids_in.reshape(sources, TOK_DEV, TOP).astype(jnp.int32)
    table = (ids_block[..., None] == jnp.arange(EXPERTS, dtype=jnp.int32)).astype(jnp.int32)
    counts = jnp.sum(table, axis=2)
    before = jnp.cumsum(counts, axis=1) - counts
    slots = jnp.sum(before[:, :, None, :] * table, axis=3)
    source_ids = jnp.arange(sources, dtype=jnp.int32)[:, None, None]
    target = ((ids_block * sources + source_ids) * CAP + slots).reshape(-1).astype(jnp.int32)
    total = EXPERTS * sources * CAP
    spread_acts = jnp.broadcast_to(acts_in[:, None, :], (TOKENS, TOP, D)).reshape(-1, D)
    spread_grads = jnp.broadcast_to(grad_in[:, None, :], (TOKENS, TOP, D)).reshape(-1, D)
    token_buf = jnp.zeros((total, D), jnp.bfloat16).at[target].set(spread_acts)
    grad_buf = jnp.zeros((total, D), jnp.bfloat16).at[target].set(spread_grads)
    gate_buf = jnp.zeros((total,), jnp.bfloat16).at[target].set(gates_in.reshape(-1))
    per_expert = sources * CAP
    outputs = lax.map(expert_backward, (token_buf.reshape(EXPERTS, per_expert, D), grad_buf.reshape(EXPERTS, per_expert, D), gate_buf.reshape(EXPERTS, per_expert), w_first_all, w_third_all, w_second_all))
    row_grads, gate_sums, grad_first, grad_third, grad_second = outputs
    returned = row_grads.reshape(total, D)[target].reshape(TOKENS, TOP, D).astype(jnp.float32)
    new_grad = (grad_in.astype(jnp.float32) + jnp.sum(returned, axis=1)).astype(jnp.bfloat16)
    gate_back = gate_sums.reshape(total)[target].reshape(TOKENS, TOP).astype(jnp.float32)
    return new_grad, gate_back, grad_first, grad_third, grad_second


def reference(acts, out_grad, expert_ids, gates, w_gate, w_up, w_down):
    act_out = jnp.zeros((SEGMENTS, MB, TOKENS, D), jnp.bfloat16)
    gate_out = jnp.zeros((SEGMENTS, MB, TOKENS, TOP), jnp.float32)
    sum_first = jnp.zeros((SEGMENTS, EXPERTS, D, HID), jnp.float32)
    sum_third = jnp.zeros((SEGMENTS, EXPERTS, D, HID), jnp.float32)
    sum_second = jnp.zeros((SEGMENTS, EXPERTS, HID, D), jnp.float32)
    for micro_index in range(MB):
        incoming = out_grad[micro_index]
        for segment_index in reversed(range(SEGMENTS)):
            result = layer_backward(acts[segment_index, micro_index], incoming, expert_ids[segment_index, micro_index], gates[segment_index, micro_index], w_gate[segment_index], w_up[segment_index], w_down[segment_index])
            act_out = act_out.at[segment_index, micro_index].set(result[0])
            gate_out = gate_out.at[segment_index, micro_index].set(result[1])
            sum_first = sum_first.at[segment_index].add(result[2])
            sum_third = sum_third.at[segment_index].add(result[3])
            sum_second = sum_second.at[segment_index].add(result[4])
            incoming = result[0]
    return act_out, gate_out, sum_first.astype(jnp.bfloat16), sum_third.astype(jnp.bfloat16), sum_second.astype(jnp.bfloat16)
```

```python
import functools

import jax
import jax.numpy as jnp
from jax import lax
from jax.experimental import pallas as pl
from jax.experimental.pallas import tpu as pltpu
from jax.sharding import PartitionSpec as P

MESH = pl.DeviceIdType.MESH
LANES = 128
ROWS = 16
TILE = 256
ROOM = 44 << 20
CONTRACT_ROWS = (((0,), (0,)), ((), ()))
CONTRACT_COLS = (((1,), (1,)), ((), ()))


def relay_kernel(
    segments, n_expert, n_fsdp,
    acts, out_grad, ids, gates, w_gate, w_up, w_down,
    act_out, gate_out, x_out, g_out, da_out, db_out, hg_out,
    wg, wu, wd, xbuf, gbuf, rbuf, zbuf, rst, zst, newg,
    slope_buf, act_buf, hid_buf, da, db, hg,
    w_sem, out_sem, xs, xr, os, gr, ds, rs, rr, zs, zr,
):
    group = n_expert * n_fsdp
    micros, toks, width = acts.shape[1:]
    hid = wg.shape[1]
    rows = group * toks
    last = segments - 1
    seg = lax.axis_index("segment")
    expert = lax.axis_index("expert")
    me = expert * n_fsdp + lax.axis_index("fsdp")
    is_last = seg == last
    tiles = [(s, min(TILE, hid - s)) for s in range(0, hid, TILE)]
    d_tiles = [(s, min(TILE, width - s)) for s in range(0, width, TILE)]

    def at(layer, member):
        return (layer, member // n_fsdp, member % n_fsdp)

    def others(fn):
        def body(i, carry):
            fn((me + i) % group)
            return carry
        lax.fori_loop(1, group, body, 0)

    def members(fn):
        def body(i, carry):
            fn((me + i) % group)
            return carry
        lax.fori_loop(0, group, body, 0)

    loads = [
        pltpu.make_async_copy(src.at[0, 0], dst, w_sem.at[i])
        for i, (src, dst) in enumerate(((w_gate, wg), (w_up, wu), (w_down, wd)))
    ]
    for load in loads:
        load.start()

    barrier = pltpu.get_barrier_semaphore()

    def greet(layer):
        def go(j):
            pl.semaphore_signal(barrier, inc=1, device_id=at(layer, j), device_id_type=MESH)
        return go

    others(greet(seg))

    @pl.when(seg > 0)
    def _():
        members(greet(seg - 1))

    @pl.when(seg < last)
    def _():
        members(greet(seg + 1))

    lane = lax.broadcasted_iota(jnp.int32, (toks, LANES), 1)
    for m in range(micros):
        xbuf[m, me, :, :width] = acts[0, m]
        named = ids[0, m]
        weight = gates[0, m].astype(jnp.float32)
        spread = jnp.zeros((toks, LANES), jnp.float32)
        for k in range(named.shape[1]):
            spread = spread + jnp.where(named[:, k : k + 1] == lane, weight[:, k : k + 1], 0.0)
        xbuf[m, me, :, width:] = spread.astype(jnp.bfloat16)

    @pl.when(is_last)
    def _():
        for m in range(micros):
            gbuf[m, me] = out_grad[m]

    below, above = (seg + last) // segments, (2 * last - seg) // segments
    pl.semaphore_wait(barrier, group - 1 + group * below + group * above)

    def x_copy(m, block, j):
        return pltpu.make_async_remote_copy(
            xbuf.at[m, block], xbuf.at[m, block], xs.at[m, j], xr.at[m, block],
            device_id=at(seg, j), device_id_type=MESH)

    def own_copy(m, block, j):
        return pltpu.make_async_remote_copy(
            gbuf.at[m, block], gbuf.at[m, block], os.at[m, j], gr.at[m, block],
            device_id=at(seg, j), device_id_type=MESH)

    def down_copy(m, block, j):
        return pltpu.make_async_remote_copy(
            newg.at[m], gbuf.at[m, block], ds.at[m, j], gr.at[m, block],
            device_id=at(lax.max(seg - 1, 0), j), device_id_type=MESH)

    def r_copy(m, block, j):
        return pltpu.make_async_remote_copy(
            rst.at[m, j], rbuf.at[m, block], rs.at[m, j], rr.at[m, block],
            device_id=at(seg, j), device_id_type=MESH)

    def z_copy(block, j):
        return pltpu.make_async_remote_copy(
            zst.at[j], zbuf.at[block], zs.at[j], zr.at[block],
            device_id=at(seg, j), device_id_type=MESH)

    for m in range(micros):
        others(lambda j: x_copy(m, me, j).start())

        @pl.when(is_last)
        def _():
            others(lambda j: own_copy(m, me, j).start())

    stores = []

    def keep(src, dst):
        copy = pltpu.make_async_copy(src, dst, out_sem.at[len(stores)])
        copy.start()
        stores.append(copy)

    def prepare(m):
        others(lambda j: x_copy(m, j, j).wait_recv())
        x = xbuf[m, :, :, :width].reshape(rows, width)
        weights = xbuf[m, :, :, width:].reshape(rows, LANES).astype(jnp.float32)
        mine = lax.broadcasted_iota(jnp.int32, (rows, LANES), 1) == expert
        c = jnp.sum(jnp.where(mine, weights, 0.0), axis=1, keepdims=True)
        for s, size in tiles:
            cut = slice(s, s + size)
            a = jnp.dot(x, wg[:, cut], preferred_element_type=jnp.float32)
            b = jnp.dot(x, wu[:, cut], preferred_element_type=jnp.float32)
            sigmoid = jax.nn.sigmoid(a)
            silu = a * sigmoid
            hidden = silu * b
            slope_buf[m, :, cut] = c * b * (sigmoid * (1.0 + a * (1.0 - sigmoid)))
            act_buf[m, :, cut] = c * silu
            hid_buf[m, :, cut] = hidden
            hg[m, :, cut] = (hidden * c).astype(jnp.bfloat16)

    def partial(m):
        others(lambda j: own_copy(m, j, j).wait_recv())

        @pl.when(seg < last)
        def _():
            own_copy(m, me, me).wait_recv()

        g = gbuf[m].reshape(rows, width)
        z = jnp.zeros((rows, 1), jnp.float32)
        for s, size in tiles:
            cut = slice(s, s + size)
            q = lax.dot_general(g, wd[cut, :], CONTRACT_COLS, preferred_element_type=jnp.float32)
            da[m, :, cut] = (q * slope_buf[m, :, cut]).astype(jnp.bfloat16)
            db[m, :, cut] = (q * act_buf[m, :, cut]).astype(jnp.bfloat16)
            z = z + jnp.sum(q * hid_buf[m, :, cut], axis=1, keepdims=True)
        for s, size in d_tiles:
            cut = slice(s, s + size)
            r = lax.dot_general(da[m], wg[cut, :], CONTRACT_COLS, preferred_element_type=jnp.float32)
            r = r + lax.dot_general(db[m], wu[cut, :], CONTRACT_COLS, preferred_element_type=jnp.float32)
            rst[m, :, :, cut] = r.astype(jnp.bfloat16).reshape(group, toks, size)
        rbuf[m, me] = rst[m, me]
        others(lambda j: r_copy(m, me, j).start())
        zst[:, m] = jnp.broadcast_to(z, (rows, LANES)).astype(jnp.bfloat16).reshape(group, toks, LANES)

    def combine(m):
        others(lambda j: r_copy(m, j, j).wait_recv())
        total = gbuf[m, me].astype(jnp.float32)
        for e in range(n_expert):
            part = rbuf[m, e * n_fsdp].astype(jnp.float32)
            for f in range(1, n_fsdp):
                part = part + rbuf[m, e * n_fsdp + f].astype(jnp.float32)
            total = total + part.astype(jnp.bfloat16).astype(jnp.float32)
        fresh = total.astype(jnp.bfloat16)
        newg[m] = fresh

        @pl.when(seg > 0)
        def _():
            members(lambda j: down_copy(m, me, j).start())

        act_out[0, m] = fresh

    for load in loads:
        load.wait()
    prepare(0)

    @pl.when(seg < last)
    def _():
        for m in range(1, micros):
            prepare(m)

    for m in range(micros):
        if m > 0:
            @pl.when(is_last)
            def _():
                prepare(m)
        partial(m)
    for m in range(micros):
        combine(m)

    zbuf[me] = zst[me]
    others(lambda j: z_copy(me, j).start())
    for m in range(micros):
        keep(xbuf.at[m, :, :, pl.ds(0, width)], x_out.at[m])
        keep(gbuf.at[m], g_out.at[m])
        keep(da.at[m], da_out.at[m])
        keep(db.at[m], db_out.at[m])
        keep(hg.at[m], hg_out.at[m])
    others(lambda j: z_copy(j, j).wait_recv())
    for m in range(micros):
        named = ids[0, m]
        total = jnp.zeros(named.shape, jnp.float32)
        for e in range(n_expert):
            part = zbuf[e * n_fsdp, m].astype(jnp.float32)
            for f in range(1, n_fsdp):
                part = part + zbuf[e * n_fsdp + f, m].astype(jnp.float32)
            part = part.astype(jnp.bfloat16).astype(jnp.float32)
            total = total + jnp.where(named == e, part[:, : named.shape[1]], 0.0)
        gate_out[0, m] = total

    for m in range(micros):
        others(lambda j: x_copy(m, me, j).wait_send())
        others(lambda j: r_copy(m, me, j).wait_send())

        @pl.when(is_last)
        def _():
            others(lambda j: own_copy(m, me, j).wait_send())

        @pl.when(seg > 0)
        def _():
            members(lambda j: down_copy(m, me, j).wait_send())
    others(lambda j: z_copy(me, j).wait_send())
    for copy in stores:
        copy.wait()


def relay_room(acts, w_gate, group):
    micros, toks, width = acts.shape[1:]
    hid = w_gate.shape[3]
    rows = micros * group * toks
    return 3 * width * hid * 2 + rows * (width * 2 * 4 + hid * (3 * 4 + 3 * 2) + LANES * 6)


def relay(acts, out_grad, ids, gates, w_gate, w_up, w_down):
    segments = lax.axis_size("segment")
    n_expert = lax.axis_size("expert")
    n_fsdp = lax.axis_size("fsdp")
    group = n_expert * n_fsdp
    micros, toks, width = acts.shape[1:]
    hid = w_gate.shape[3]
    fits = (
        toks % ROWS == 0
        and width % LANES == 0
        and hid % LANES == 0
        and n_expert <= LANES
        and relay_room(acts, w_gate, group) <= ROOM
    )
    if not fits:
        return local(acts, out_grad, ids, gates, w_gate, w_up, w_down)
    rows = group * toks
    bf16, f32 = jnp.bfloat16, jnp.float32
    vmem = pl.BlockSpec(memory_space=pltpu.VMEM)
    far = pl.BlockSpec(memory_space=pl.ANY)
    dma = pltpu.SemaphoreType.DMA
    scratch = [
        pltpu.VMEM((width, hid), bf16),
        pltpu.VMEM((width, hid), bf16),
        pltpu.VMEM((hid, width), bf16),
        pltpu.VMEM((micros, group, toks, width + LANES), bf16),
        pltpu.VMEM((micros, group, toks, width), bf16),
        pltpu.VMEM((micros, group, toks, width), bf16),
        pltpu.VMEM((group, micros, toks, LANES), bf16),
        pltpu.VMEM((micros, group, toks, width), bf16),
        pltpu.VMEM((group, micros, toks, LANES), bf16),
        pltpu.VMEM((micros, toks, width), bf16),
    ]
    scratch += [pltpu.VMEM((micros, rows, hid), f32)] * 3
    scratch += [pltpu.VMEM((micros, rows, hid), bf16)] * 3
    scratch += [dma((3,)), dma((5 * micros,))]
    scratch += [dma((micros, group))] * 7
    scratch += [dma((group,))] * 2
    flops = 2 * micros * rows * width * hid * 5
    outs = pl.pallas_call(
        functools.partial(relay_kernel, segments, n_expert, n_fsdp),
        out_shape=(
            jax.ShapeDtypeStruct(acts.shape, bf16),
            jax.ShapeDtypeStruct(gates.shape, f32),
            jax.ShapeDtypeStruct((micros, group, toks, width), bf16),
            jax.ShapeDtypeStruct((micros, group, toks, width), bf16),
            jax.ShapeDtypeStruct((micros, rows, hid), bf16),
            jax.ShapeDtypeStruct((micros, rows, hid), bf16),
            jax.ShapeDtypeStruct((micros, rows, hid), bf16),
        ),
        in_specs=[vmem, vmem, vmem, vmem, far, far, far],
        out_specs=(vmem, vmem, far, far, far, far, far),
        scratch_shapes=scratch,
        compiler_params=pltpu.CompilerParams(
            collective_id=0, has_side_effects=True, vmem_limit_bytes=ROOM + (8 << 20)
        ),
        cost_estimate=pl.CostEstimate(
            flops=flops, bytes_accessed=6 * width * hid, transcendentals=micros * rows * hid
        ),
    )(acts, out_grad, ids, gates, w_gate, w_up, w_down)
    act_grad, gate_grad, x, g, da, db, hg = outs
    x = x.reshape(-1, width)
    g = g.reshape(-1, width)

    def weight_grad(left, right):
        total = lax.dot_general(left, right, CONTRACT_ROWS, preferred_element_type=f32)
        return total.astype(bf16)[None, None]

    da, db, hg = (v.reshape(-1, hid) for v in (da, db, hg))
    return act_grad, gate_grad, weight_grad(x, da), weight_grad(x, db), weight_grad(hg, g)


def from_behind(value, axis, steps):
    count = lax.axis_size(axis)
    leading, last = (max(0, -steps), min(count, count - steps))
    return lax.ppermute(value, axis, [(source, source + steps) for source in range(leading, last)])


def silu_parts(pre_gate):
    sigmoid = jax.nn.sigmoid(pre_gate)
    return (pre_gate * sigmoid, sigmoid * (1.0 + pre_gate * (1.0 - sigmoid)))


def local(acts, out_grad, expert_ids, gates, w_gate, w_up, w_down):
    segments = lax.axis_size("segment")
    segment_now = lax.axis_index("segment")
    n_expert = lax.axis_size("expert")
    n_fsdp = lax.axis_size("fsdp")
    micro_count = acts.shape[1]
    tok_count = acts.shape[2]
    width = acts.shape[3]
    top_count = expert_ids.shape[3]
    capacity = 5 * top_count * tok_count // (4 * n_expert)
    w_first = w_gate[0, 0]
    w_third = w_up[0, 0]
    w_second = w_down[0, 0]
    hid_local = w_first.shape[1]
    expert_iota = jnp.arange(n_expert, dtype=jnp.int32)
    slot_iota = jnp.arange(capacity, dtype=jnp.int32)
    micro_iota = jnp.arange(micro_count, dtype=jnp.int32)
    contract_rows = (((0,), (0,)), ((), ()))
    contract_cols = (((1,), (1,)), ((), ()))
    grad_first = jnp.zeros((width, hid_local), jnp.float32)
    grad_third = jnp.zeros((width, hid_local), jnp.float32)
    grad_second = jnp.zeros((hid_local, width), jnp.float32)
    act_out = jnp.zeros(acts.shape, jnp.bfloat16)
    gate_out = jnp.zeros(gates.shape, jnp.float32)
    previous = jnp.zeros((tok_count, width), jnp.bfloat16)
    for moment in range(micro_count + segments - 1):
        micro_index = moment - (segments - 1 - segment_now)
        valid = (micro_index >= 0) & (micro_index < micro_count)
        picked = jnp.clip(micro_index, 0, micro_count - 1)
        tokens_now = lax.dynamic_index_in_dim(acts[0], picked, 0, keepdims=False)
        loss_grad = lax.dynamic_index_in_dim(out_grad, picked, 0, keepdims=False)
        ids_now = lax.dynamic_index_in_dim(expert_ids[0], picked, 0, keepdims=False)
        gates_now = lax.dynamic_index_in_dim(gates[0], picked, 0, keepdims=False)
        if moment > 0:
            incoming = from_behind(previous, "segment", -1)
        else:
            incoming = previous
        grad_now = jnp.where(segment_now == segments - 1, loss_grad, incoming)
        table = (ids_now[:, :, None] == expert_iota).astype(jnp.int32)
        counts = jnp.sum(table, axis=1)
        before = jnp.cumsum(counts, axis=0) - counts
        slots = jnp.sum(before[:, None, :] * table, axis=2)
        routing = (
            (ids_now[None, None] == expert_iota[:, None, None, None])
            & (slots[None, None] == slot_iota[None, :, None, None])
        ).astype(jnp.float32)
        placing = jnp.sum(routing, axis=3).astype(jnp.bfloat16)
        token_buf = jnp.einsum(
            "ect,td->ecd", placing, tokens_now, preferred_element_type=jnp.float32
        ).astype(jnp.bfloat16)
        grad_buf = jnp.einsum(
            "ect,td->ecd", placing, grad_now, preferred_element_type=jnp.float32
        ).astype(jnp.bfloat16)
        gate_buf = jnp.einsum("ectk,tk->ec", routing, gates_now.astype(jnp.float32)).astype(
            jnp.bfloat16
        )
        start_state = (
            grad_first,
            grad_third,
            grad_second,
            jnp.zeros((n_fsdp, n_expert, capacity, width), jnp.bfloat16),
            jnp.zeros((n_fsdp, n_expert, capacity), jnp.bfloat16),
        )
        grouped = (
            lax.all_gather(token_buf[None], "fsdp", axis=0, tiled=True),
            lax.all_gather(grad_buf[None], "fsdp", axis=0, tiled=True),
            lax.all_gather(gate_buf[None], "fsdp", axis=0, tiled=True),
        )
        token_rows = lax.all_to_all(grouped[0], "expert", split_axis=1, concat_axis=1, tiled=True)
        grad_rows = lax.all_to_all(grouped[1], "expert", split_axis=1, concat_axis=1, tiled=True)
        gate_rows = lax.all_to_all(grouped[2], "expert", split_axis=1, concat_axis=1, tiled=True)

        def compute(state):
            sum_first, sum_third, sum_second, part_rows, part_gates = state
            flat_tokens = token_rows.reshape(-1, width)
            flat_grads = grad_rows.reshape(-1, width)
            gate_col = gate_rows.reshape(-1).astype(jnp.float32)[:, None]
            pre_gate = jnp.dot(flat_tokens, w_first, preferred_element_type=jnp.float32)
            pre_up = jnp.dot(flat_tokens, w_third, preferred_element_type=jnp.float32)
            activated, slope_term = silu_parts(pre_gate)
            hidden = activated * pre_up
            back_hidden = lax.dot_general(
                flat_grads, w_second, contract_cols, preferred_element_type=jnp.float32
            )
            scaled = back_hidden * gate_col
            grad_gate_pre = (scaled * pre_up * slope_term).astype(jnp.bfloat16)
            grad_up_pre = (scaled * activated).astype(jnp.bfloat16)
            hidden_gated = (hidden * gate_col).astype(jnp.bfloat16)
            sum_first = sum_first + lax.dot_general(
                flat_tokens, grad_gate_pre, contract_rows, preferred_element_type=jnp.float32
            )
            sum_third = sum_third + lax.dot_general(
                flat_tokens, grad_up_pre, contract_rows, preferred_element_type=jnp.float32
            )
            sum_second = sum_second + lax.dot_general(
                hidden_gated, flat_grads, contract_rows, preferred_element_type=jnp.float32
            )
            partial_value = lax.dot_general(
                grad_gate_pre, w_first, contract_cols, preferred_element_type=jnp.float32
            )
            partial_value = partial_value + lax.dot_general(
                grad_up_pre, w_third, contract_cols, preferred_element_type=jnp.float32
            )
            gate_part = jnp.sum(hidden * back_hidden, axis=1)
            part_rows = partial_value.astype(jnp.bfloat16).reshape(token_rows.shape)
            part_gates = gate_part.astype(jnp.bfloat16).reshape(gate_rows.shape)
            return (sum_first, sum_third, sum_second, part_rows, part_gates)

        finished = lax.cond(valid, compute, lambda state: state, start_state)
        grad_first, grad_third, grad_second, part_rows, part_gates = finished
        summed_rows, summed_gates = (
            lax.psum_scatter(part_rows, "fsdp", scatter_dimension=0, tiled=True).astype(
                jnp.float32
            ),
            lax.psum_scatter(part_gates, "fsdp", scatter_dimension=0, tiled=True).astype(
                jnp.float32
            ),
        )
        back_rows, back_gates = (
            lax.all_to_all(
                summed_rows[0].astype(jnp.bfloat16),
                "expert",
                split_axis=0,
                concat_axis=0,
                tiled=True,
            ),
            lax.all_to_all(
                summed_gates[0].astype(jnp.bfloat16),
                "expert",
                split_axis=0,
                concat_axis=0,
                tiled=True,
            ),
        )
        token_back = jnp.einsum(
            "ect,ecd->td", placing, back_rows, preferred_element_type=jnp.float32
        )
        new_grad = (grad_now.astype(jnp.float32) + token_back).astype(jnp.bfloat16)
        gate_new = jnp.einsum("ectk,ec->tk", routing, back_gates.astype(jnp.float32))
        chosen = micro_iota == micro_index
        act_out = jnp.where(chosen[None, :, None, None], new_grad[None, None], act_out)
        gate_out = jnp.where(chosen[None, :, None, None], gate_new[None, None], gate_out)
        previous = new_grad
    return (
        act_out,
        gate_out,
        grad_first.astype(jnp.bfloat16)[None, None],
        grad_third.astype(jnp.bfloat16)[None, None],
        grad_second.astype(jnp.bfloat16)[None, None],
    )


def solution(mesh):
    in_specs = (
        P("segment", None, ("expert", "fsdp"), None),
        P(None, ("expert", "fsdp"), None),
        P("segment", None, ("expert", "fsdp"), None),
        P("segment", None, ("expert", "fsdp"), None),
        P("segment", "expert", None, "fsdp"),
        P("segment", "expert", None, "fsdp"),
        P("segment", "expert", "fsdp", None),
    )
    out_specs = (
        P("segment", None, ("expert", "fsdp"), None),
        P("segment", None, ("expert", "fsdp"), None),
        P("segment", "expert", None, "fsdp"),
        P("segment", "expert", None, "fsdp"),
        P("segment", "expert", "fsdp", None),
    )
    return jax.shard_map(relay, mesh=mesh, in_specs=in_specs, out_specs=out_specs, check_vma=False)
```

```python
import functools

import jax
import jax.numpy as jnp
from jax import lax
from jax.experimental import pallas as pl
from jax.experimental.pallas import tpu as pltpu
from jax.sharding import PartitionSpec as P

MESH = pl.DeviceIdType.MESH
LANES = 128
ROWS = 16
TILE = 256
GRANT = 62 << 20
ROOM = 44 << 20
PARTS = 2
CONTRACT_COLS = (((1,), (1,)), ((), ()))


def relay_kernel(
    segments, n_expert, n_fsdp,
    acts, out_grad, ids, gates, w_gate, w_up, w_down,
    act_out, gate_out, xt_out, g_out, da_out, db_out, hgt_out,
    wg, wu, wd, xbuf, gbuf, rbuf, zbuf, rst, zst, newg,
    slope_buf, act_buf, hid_buf, qbuf, da, db, hg, xt, hgt,
    in_sem, out_sem, go, xs, xr, os, gr, ds, rs, rr, zs, zr,
):
    group = n_expert * n_fsdp
    micros, toks, width = acts.shape[1:]
    hid = wg.shape[1]
    rows = group * toks
    last = segments - 1
    part_width = newg.shape[2]
    parts = width // part_width
    seg = lax.axis_index("segment")
    expert = lax.axis_index("expert")
    fsdp = lax.axis_index("fsdp")
    me = expert * n_fsdp + fsdp
    is_last = seg == last
    tiles = [(s, min(TILE, hid - s)) for s in range(0, hid, TILE)]
    d_tiles = [(s, min(TILE, part_width - s)) for s in range(0, part_width, TILE)]

    def at(layer, member):
        return (layer, member // n_fsdp, member % n_fsdp)

    def turn_round(first, count, start, fn):
        def body(i, carry):
            fn((start + i) % count)
            return carry
        lax.fori_loop(first, count, body, 0)

    def others(fn):
        turn_round(1, group, me, fn)

    def members(fn):
        turn_round(0, group, me, fn)

    def other_experts(fn):
        turn_round(1, n_expert, expert, fn)

    def other_fsdp(fn):
        turn_round(1, n_fsdp, fsdp, fn)

    def own_loss(m, c):
        return pltpu.make_async_copy(
            out_grad.at[m, :, pl.ds(c * part_width, part_width)], gbuf.at[m * parts + c, me],
            in_sem.at[3 + micros + m * parts + c])

    own_acts = [
        pltpu.make_async_copy(acts.at[0, m], xbuf.at[m, me, :, pl.ds(0, width)], in_sem.at[3 + m])
        for m in range(micros)
    ]
    for copy in own_acts:
        copy.start()

    @pl.when(is_last)
    def _():
        for m in range(micros):
            for c in range(parts):
                own_loss(m, c).start()

    loads = [
        pltpu.make_async_copy(src.at[0, 0], dst, in_sem.at[i])
        for i, (src, dst) in enumerate(((w_gate, wg), (w_up, wu), (w_down, wd)))
    ]
    for load in loads:
        load.start()

    barrier = pltpu.get_barrier_semaphore()

    def greet(layer):
        def tell(j):
            pl.semaphore_signal(barrier, inc=1, device_id=at(layer, j), device_id_type=MESH)
        return tell

    others(greet(seg))

    @pl.when(seg > 0)
    def _():
        members(greet(seg - 1))

    @pl.when(seg < last)
    def _():
        members(greet(seg + 1))

    lane = lax.broadcasted_iota(jnp.int32, (toks, LANES), 1)
    for m in range(micros):
        named = ids[0, m].T
        weight = gates[0, m].astype(jnp.float32).T
        spread = jnp.zeros((toks, LANES), jnp.float32)
        for k in range(named.shape[1]):
            spread = spread + jnp.where(named[:, k : k + 1] == lane, weight[:, k : k + 1], 0.0)
        xbuf[m, me, :, width:] = spread.astype(jnp.bfloat16)

    below, above = (seg + last) // segments, (2 * last - seg) // segments
    pl.semaphore_wait(barrier, group - 1 + group * below + group * above)

    def x_copy(p, block, j, slot):
        return pltpu.make_async_remote_copy(
            xbuf.at[p, block], xbuf.at[p, block], xs.at[p, slot], xr.at[p, block],
            device_id=at(seg, j), device_id_type=MESH)

    def own_copy(p, block, j, slot):
        return pltpu.make_async_remote_copy(
            gbuf.at[p, block], gbuf.at[p, block], os.at[p, slot], gr.at[p, block],
            device_id=at(seg, j), device_id_type=MESH)

    def down_copy(p, block, j):
        return pltpu.make_async_remote_copy(
            newg.at[p], gbuf.at[p, block], ds.at[p, j], gr.at[p, block],
            device_id=at(lax.max(seg - 1, 0), j), device_id_type=MESH)

    def r_copy(p, block, j):
        return pltpu.make_async_remote_copy(
            rst.at[p, j], rbuf.at[p, block], rs.at[p, j], rr.at[p, block],
            device_id=at(seg, j), device_id_type=MESH)

    def z_copy(block, j):
        return pltpu.make_async_remote_copy(
            zst.at[j], zbuf.at[block], zs.at[j], zr.at[block],
            device_id=at(seg, j), device_id_type=MESH)

    def spread_own(copy, p):
        def along(e):
            j = e * n_fsdp + fsdp
            copy(p, me, j, j).start()

        def across(f):
            j = expert * n_fsdp + f
            copy(p, me, j, j).start()

        other_experts(along)
        other_fsdp(across)

    def pass_on(copy, p):
        def along(e):
            block = e * n_fsdp + fsdp
            copy(p, block, block, block).wait_recv()

            def across(f):
                copy(p, block, expert * n_fsdp + f, e * n_fsdp + f).start()

            other_fsdp(across)

        other_experts(along)

    def take_rest(copy, p):
        def across(f):
            def along(e, carry):
                block = e * n_fsdp + f
                copy(p, block, block, block).wait_recv()
                return carry
            lax.fori_loop(0, n_expert, along, 0)
        other_fsdp(across)

    def spread_sent(copy, p):
        others(lambda j: copy(p, me, j, j).wait_send())

    def pieces(m):
        return range(m * parts, (m + 1) * parts)

    def send_loss(m):
        for c in range(parts):
            own_loss(m, c).wait()
        for p in pieces(m):
            spread_own(own_copy, p)

    def pass_loss(m):
        for p in pieces(m):
            pass_on(own_copy, p)

    def allow_next():
        @pl.when(seg > 0)
        def _():
            pl.semaphore_signal(go, inc=1, device_id=at(seg - 1, me), device_id_type=MESH)

    for copy in own_acts:
        copy.wait()

    @pl.when(is_last)
    def _():
        spread_own(x_copy, 0)
        send_loss(0)
        pass_on(x_copy, 0)
        pass_loss(0)
        for m in range(1, micros):
            spread_own(x_copy, m)
            send_loss(m)
        take_rest(x_copy, 0)
        allow_next()

    @pl.when(seg < last)
    def _():
        pl.semaphore_wait(go, 1)
        for m in range(micros):
            spread_own(x_copy, m)
        for m in range(micros):
            pass_on(x_copy, m)
        for m in range(micros):
            take_rest(x_copy, m)
        allow_next()

    stores = []

    def keep(src, dst):
        copy = pltpu.make_async_copy(src, dst, out_sem.at[len(stores)])
        copy.start()
        stores.append(copy)

    def prepare(m):
        x = xbuf[m, :, :, :width].reshape(rows, width)
        weights = xbuf[m, :, :, width:].reshape(rows, LANES).astype(jnp.float32)
        mine = lax.broadcasted_iota(jnp.int32, (rows, LANES), 1) == expert
        c = jnp.sum(jnp.where(mine, weights, 0.0), axis=1, keepdims=True)
        for s, size in tiles:
            cut = slice(s, s + size)
            a = jnp.dot(x, wg[:, cut], preferred_element_type=jnp.float32)
            b = jnp.dot(x, wu[:, cut], preferred_element_type=jnp.float32)
            sigmoid = jax.nn.sigmoid(a)
            silu = a * sigmoid
            hidden = silu * b
            slope_buf[m, :, cut] = c * b * (sigmoid * (1.0 + a * (1.0 - sigmoid)))
            act_buf[m, :, cut] = c * silu
            hid_buf[m, :, cut] = hidden
            hg[m, :, cut] = (hidden * c).astype(jnp.bfloat16)

    def transpose(m):
        cut = slice(m * rows, (m + 1) * rows)
        xt[:, cut] = xbuf[m, :, :, :width].reshape(rows, width).T
        hgt[:, cut] = hg[m].T

    def partial(m):
        z = jnp.zeros((rows, 1), jnp.float32)
        for c, p in enumerate(pieces(m)):
            @pl.when(is_last)
            def _():
                take_rest(own_copy, p)

            @pl.when(seg < last)
            def _():
                members(lambda j: own_copy(p, j, j, j).wait_recv())

            g = gbuf[p].reshape(rows, part_width)
            columns = slice(c * part_width, (c + 1) * part_width)
            for s, size in tiles:
                cut = slice(s, s + size)
                q = lax.dot_general(
                    g, wd[cut, columns], CONTRACT_COLS, preferred_element_type=jnp.float32)
                if c > 0:
                    q = q + qbuf[:, cut]
                if c < parts - 1:
                    qbuf[:, cut] = q
                else:
                    da[m, :, cut] = (q * slope_buf[m, :, cut]).astype(jnp.bfloat16)
                    db[m, :, cut] = (q * act_buf[m, :, cut]).astype(jnp.bfloat16)
                    z = z + jnp.sum(q * hid_buf[m, :, cut], axis=1, keepdims=True)
        for c, p in enumerate(pieces(m)):
            for s, size in d_tiles:
                cut = slice(c * part_width + s, c * part_width + s + size)
                r = lax.dot_general(
                    da[m], wg[cut, :], CONTRACT_COLS, preferred_element_type=jnp.float32)
                r = r + lax.dot_general(
                    db[m], wu[cut, :], CONTRACT_COLS, preferred_element_type=jnp.float32)
                rst[p, :, :, s : s + size] = r.astype(jnp.bfloat16).reshape(group, toks, size)
            others(lambda j: r_copy(p, me, j).start())
            rbuf[p, me] = rst[p, me]
        zst[:, m] = jnp.broadcast_to(z, (rows, LANES)).astype(jnp.bfloat16).reshape(group, toks, LANES)

    def combine(m):
        for c, p in enumerate(pieces(m)):
            others(lambda j: r_copy(p, j, j).wait_recv())
            total = gbuf[p, me].astype(jnp.float32)
            for e in range(n_expert):
                part = rbuf[p, e * n_fsdp].astype(jnp.float32)
                for f in range(1, n_fsdp):
                    part = part + rbuf[p, e * n_fsdp + f].astype(jnp.float32)
                total = total + part.astype(jnp.bfloat16).astype(jnp.float32)
            fresh = total.astype(jnp.bfloat16)
            newg[p] = fresh

            @pl.when(seg > 0)
            def _():
                members(lambda j: down_copy(p, me, j).start())

            act_out[0, m, :, c * part_width : (c + 1) * part_width] = fresh

    for load in loads:
        load.wait()
    prepare(0)

    @pl.when(seg < last)
    def _():
        for m in range(1, micros):
            prepare(m)

    @pl.when(seg == 0)
    def _():
        for m in range(micros):
            if m > 0 and segments == 1:
                continue
            transpose(m)

    for m in range(micros):
        if m > 0:
            @pl.when(is_last)
            def _():
                pass_on(x_copy, m)
                pass_loss(m)
                take_rest(x_copy, m)
                prepare(m)
        partial(m)

    zbuf[me] = zst[me]
    others(lambda j: z_copy(me, j).start())
    for m in range(micros):
        for c, p in enumerate(pieces(m)):
            keep(gbuf.at[p], g_out.at[m, :, :, pl.ds(c * part_width, part_width)])
        keep(da.at[m], da_out.at[m])
        keep(db.at[m], db_out.at[m])
    for m in range(micros):
        combine(m)

    @pl.when((seg > 0) | (segments == 1))
    def _():
        for m in range(micros):
            transpose(m)

    keep(xt, xt_out)
    keep(hgt, hgt_out)
    others(lambda j: z_copy(j, j).wait_recv())
    for m in range(micros):
        named = ids[0, m].T
        total = jnp.zeros(named.shape, jnp.float32)
        for e in range(n_expert):
            part = zbuf[e * n_fsdp, m].astype(jnp.float32)
            for f in range(1, n_fsdp):
                part = part + zbuf[e * n_fsdp + f, m].astype(jnp.float32)
            part = part.astype(jnp.bfloat16).astype(jnp.float32)
            total = total + jnp.where(named == e, part[:, : named.shape[1]], 0.0)
        gate_out[0, m] = total.T

    for m in range(micros):
        spread_sent(x_copy, m)
        for p in pieces(m):
            others(lambda j: r_copy(p, me, j).wait_send())

            @pl.when(is_last)
            def _():
                spread_sent(own_copy, p)

            @pl.when(seg > 0)
            def _():
                members(lambda j: down_copy(p, me, j).wait_send())
    others(lambda j: z_copy(me, j).wait_send())
    for copy in stores:
        copy.wait()


def relay_room(acts, w_gate, group):
    micros, toks, width = acts.shape[1:]
    hid = w_gate.shape[3]
    rows = micros * group * toks
    return 3 * width * hid * 2 + rows * (width * 2 * 4 + hid * (4 * 4 + 4 * 2) + width * 2 + LANES * 6)


def relay(acts, out_grad, ids, gates, w_gate, w_up, w_down):
    segments = lax.axis_size("segment")
    n_expert = lax.axis_size("expert")
    n_fsdp = lax.axis_size("fsdp")
    group = n_expert * n_fsdp
    micros, toks, width = acts.shape[1:]
    hid = w_gate.shape[3]
    fits = (
        toks % ROWS == 0
        and group * toks % LANES == 0
        and width % LANES == 0
        and hid % LANES == 0
        and n_expert <= LANES
        and relay_room(acts, w_gate, group) <= ROOM
    )
    if not fits:
        return local(acts, out_grad, ids, gates, w_gate, w_up, w_down)
    rows = group * toks
    parts = PARTS if width % (PARTS * LANES) == 0 else 1
    pieces = micros * parts
    piece = (pieces, group, toks, width // parts)
    bf16, f32 = jnp.bfloat16, jnp.float32
    vmem = pl.BlockSpec(memory_space=pltpu.VMEM)
    far = pl.BlockSpec(memory_space=pl.ANY)
    home = pl.BlockSpec(memory_space=pltpu.HBM)
    dma = pltpu.SemaphoreType.DMA
    scratch = [
        pltpu.VMEM((width, hid), bf16),
        pltpu.VMEM((width, hid), bf16),
        pltpu.VMEM((hid, width), bf16),
        pltpu.VMEM((micros, group, toks, width + LANES), bf16),
        pltpu.VMEM(piece, bf16),
        pltpu.VMEM(piece, bf16),
        pltpu.VMEM((group, micros, toks, LANES), bf16),
        pltpu.VMEM(piece, bf16),
        pltpu.VMEM((group, micros, toks, LANES), bf16),
        pltpu.VMEM((pieces, toks, width // parts), bf16),
    ]
    scratch += [pltpu.VMEM((micros, rows, hid), f32)] * 3
    scratch += [pltpu.VMEM((rows, hid), f32)]
    scratch += [pltpu.VMEM((micros, rows, hid), bf16)] * 3
    scratch += [pltpu.VMEM((width, micros * rows), bf16), pltpu.VMEM((hid, micros * rows), bf16)]
    scratch += [dma((3 + micros + pieces,)), dma((2 + 2 * micros + pieces,))]
    scratch += [pltpu.SemaphoreType.REGULAR]
    scratch += [dma((micros, group))] * 2
    scratch += [dma((pieces, group))] * 5
    scratch += [dma((group,))] * 2
    flops = 2 * micros * rows * width * hid * 5
    outs = pl.pallas_call(
        functools.partial(relay_kernel, segments, n_expert, n_fsdp),
        out_shape=(
            jax.ShapeDtypeStruct(acts.shape, bf16),
            jax.ShapeDtypeStruct(gates.shape[:2] + (gates.shape[3], toks), f32),
            jax.ShapeDtypeStruct((width, micros * rows), bf16),
            jax.ShapeDtypeStruct((micros, group, toks, width), bf16),
            jax.ShapeDtypeStruct((micros, rows, hid), bf16),
            jax.ShapeDtypeStruct((micros, rows, hid), bf16),
            jax.ShapeDtypeStruct((hid, micros * rows), bf16),
        ),
        in_specs=[home, home, vmem, vmem, far, far, far],
        out_specs=(vmem, vmem, far, far, far, far, far),
        scratch_shapes=scratch,
        compiler_params=pltpu.CompilerParams(
            collective_id=0, has_side_effects=True, vmem_limit_bytes=GRANT
        ),
        cost_estimate=pl.CostEstimate(
            flops=flops, bytes_accessed=6 * width * hid, transcendentals=micros * rows * hid
        ),
    )(acts, out_grad, ids.swapaxes(2, 3), gates.swapaxes(2, 3), w_gate, w_up, w_down)
    act_grad, gate_grad, xt, g, da, db, hgt = outs

    def weight_grad(left, right):
        total = jnp.dot(left, right.reshape(micros * rows, -1), preferred_element_type=f32)
        return total.astype(bf16)[None, None]

    return act_grad, gate_grad.swapaxes(2, 3), weight_grad(xt, da), weight_grad(xt, db), weight_grad(hgt, g)


def from_behind(value, axis, steps):
    count = lax.axis_size(axis)
    leading, last = (max(0, -steps), min(count, count - steps))
    return lax.ppermute(value, axis, [(source, source + steps) for source in range(leading, last)])


def silu_parts(pre_gate):
    sigmoid = jax.nn.sigmoid(pre_gate)
    return (pre_gate * sigmoid, sigmoid * (1.0 + pre_gate * (1.0 - sigmoid)))


def local(acts, out_grad, expert_ids, gates, w_gate, w_up, w_down):
    segments = lax.axis_size("segment")
    segment_now = lax.axis_index("segment")
    n_expert = lax.axis_size("expert")
    n_fsdp = lax.axis_size("fsdp")
    micro_count = acts.shape[1]
    tok_count = acts.shape[2]
    width = acts.shape[3]
    top_count = expert_ids.shape[3]
    capacity = 5 * top_count * tok_count // (4 * n_expert)
    w_first = w_gate[0, 0]
    w_third = w_up[0, 0]
    w_second = w_down[0, 0]
    hid_local = w_first.shape[1]
    expert_iota = jnp.arange(n_expert, dtype=jnp.int32)
    slot_iota = jnp.arange(capacity, dtype=jnp.int32)
    micro_iota = jnp.arange(micro_count, dtype=jnp.int32)
    contract_rows = (((0,), (0,)), ((), ()))
    contract_cols = (((1,), (1,)), ((), ()))
    grad_first = jnp.zeros((width, hid_local), jnp.float32)
    grad_third = jnp.zeros((width, hid_local), jnp.float32)
    grad_second = jnp.zeros((hid_local, width), jnp.float32)
    act_out = jnp.zeros(acts.shape, jnp.bfloat16)
    gate_out = jnp.zeros(gates.shape, jnp.float32)
    previous = jnp.zeros((tok_count, width), jnp.bfloat16)
    for moment in range(micro_count + segments - 1):
        micro_index = moment - (segments - 1 - segment_now)
        valid = (micro_index >= 0) & (micro_index < micro_count)
        picked = jnp.clip(micro_index, 0, micro_count - 1)
        tokens_now = lax.dynamic_index_in_dim(acts[0], picked, 0, keepdims=False)
        loss_grad = lax.dynamic_index_in_dim(out_grad, picked, 0, keepdims=False)
        ids_now = lax.dynamic_index_in_dim(expert_ids[0], picked, 0, keepdims=False)
        gates_now = lax.dynamic_index_in_dim(gates[0], picked, 0, keepdims=False)
        if moment > 0:
            incoming = from_behind(previous, "segment", -1)
        else:
            incoming = previous
        grad_now = jnp.where(segment_now == segments - 1, loss_grad, incoming)
        table = (ids_now[:, :, None] == expert_iota).astype(jnp.int32)
        counts = jnp.sum(table, axis=1)
        before = jnp.cumsum(counts, axis=0) - counts
        slots = jnp.sum(before[:, None, :] * table, axis=2)
        routing = (
            (ids_now[None, None] == expert_iota[:, None, None, None])
            & (slots[None, None] == slot_iota[None, :, None, None])
        ).astype(jnp.float32)
        placing = jnp.sum(routing, axis=3).astype(jnp.bfloat16)
        token_buf = jnp.einsum(
            "ect,td->ecd", placing, tokens_now, preferred_element_type=jnp.float32
        ).astype(jnp.bfloat16)
        grad_buf = jnp.einsum(
            "ect,td->ecd", placing, grad_now, preferred_element_type=jnp.float32
        ).astype(jnp.bfloat16)
        gate_buf = jnp.einsum("ectk,tk->ec", routing, gates_now.astype(jnp.float32)).astype(
            jnp.bfloat16
        )
        start_state = (
            grad_first,
            grad_third,
            grad_second,
            jnp.zeros((n_fsdp, n_expert, capacity, width), jnp.bfloat16),
            jnp.zeros((n_fsdp, n_expert, capacity), jnp.bfloat16),
        )
        grouped = (
            lax.all_gather(token_buf[None], "fsdp", axis=0, tiled=True),
            lax.all_gather(grad_buf[None], "fsdp", axis=0, tiled=True),
            lax.all_gather(gate_buf[None], "fsdp", axis=0, tiled=True),
        )
        token_rows = lax.all_to_all(grouped[0], "expert", split_axis=1, concat_axis=1, tiled=True)
        grad_rows = lax.all_to_all(grouped[1], "expert", split_axis=1, concat_axis=1, tiled=True)
        gate_rows = lax.all_to_all(grouped[2], "expert", split_axis=1, concat_axis=1, tiled=True)

        def compute(state):
            sum_first, sum_third, sum_second, part_rows, part_gates = state
            flat_tokens = token_rows.reshape(-1, width)
            flat_grads = grad_rows.reshape(-1, width)
            gate_col = gate_rows.reshape(-1).astype(jnp.float32)[:, None]
            pre_gate = jnp.dot(flat_tokens, w_first, preferred_element_type=jnp.float32)
            pre_up = jnp.dot(flat_tokens, w_third, preferred_element_type=jnp.float32)
            activated, slope_term = silu_parts(pre_gate)
            hidden = activated * pre_up
            back_hidden = lax.dot_general(
                flat_grads, w_second, contract_cols, preferred_element_type=jnp.float32
            )
            scaled = back_hidden * gate_col
            grad_gate_pre = (scaled * pre_up * slope_term).astype(jnp.bfloat16)
            grad_up_pre = (scaled * activated).astype(jnp.bfloat16)
            hidden_gated = (hidden * gate_col).astype(jnp.bfloat16)
            sum_first = sum_first + lax.dot_general(
                flat_tokens, grad_gate_pre, contract_rows, preferred_element_type=jnp.float32
            )
            sum_third = sum_third + lax.dot_general(
                flat_tokens, grad_up_pre, contract_rows, preferred_element_type=jnp.float32
            )
            sum_second = sum_second + lax.dot_general(
                hidden_gated, flat_grads, contract_rows, preferred_element_type=jnp.float32
            )
            partial_value = lax.dot_general(
                grad_gate_pre, w_first, contract_cols, preferred_element_type=jnp.float32
            )
            partial_value = partial_value + lax.dot_general(
                grad_up_pre, w_third, contract_cols, preferred_element_type=jnp.float32
            )
            gate_part = jnp.sum(hidden * back_hidden, axis=1)
            part_rows = partial_value.astype(jnp.bfloat16).reshape(token_rows.shape)
            part_gates = gate_part.astype(jnp.bfloat16).reshape(gate_rows.shape)
            return (sum_first, sum_third, sum_second, part_rows, part_gates)

        finished = lax.cond(valid, compute, lambda state: state, start_state)
        grad_first, grad_third, grad_second, part_rows, part_gates = finished
        summed_rows, summed_gates = (
            lax.psum_scatter(part_rows, "fsdp", scatter_dimension=0, tiled=True).astype(
                jnp.float32
            ),
            lax.psum_scatter(part_gates, "fsdp", scatter_dimension=0, tiled=True).astype(
                jnp.float32
            ),
        )
        back_rows, back_gates = (
            lax.all_to_all(
                summed_rows[0].astype(jnp.bfloat16),
                "expert",
                split_axis=0,
                concat_axis=0,
                tiled=True,
            ),
            lax.all_to_all(
                summed_gates[0].astype(jnp.bfloat16),
                "expert",
                split_axis=0,
                concat_axis=0,
                tiled=True,
            ),
        )
        token_back = jnp.einsum(
            "ect,ecd->td", placing, back_rows, preferred_element_type=jnp.float32
        )
        new_grad = (grad_now.astype(jnp.float32) + token_back).astype(jnp.bfloat16)
        gate_new = jnp.einsum("ectk,ec->tk", routing, back_gates.astype(jnp.float32))
        chosen = micro_iota == micro_index
        act_out = jnp.where(chosen[None, :, None, None], new_grad[None, None], act_out)
        gate_out = jnp.where(chosen[None, :, None, None], gate_new[None, None], gate_out)
        previous = new_grad
    return (
        act_out,
        gate_out,
        grad_first.astype(jnp.bfloat16)[None, None],
        grad_third.astype(jnp.bfloat16)[None, None],
        grad_second.astype(jnp.bfloat16)[None, None],
    )


def solution(mesh):
    in_specs = (
        P("segment", None, ("expert", "fsdp"), None),
        P(None, ("expert", "fsdp"), None),
        P("segment", None, ("expert", "fsdp"), None),
        P("segment", None, ("expert", "fsdp"), None),
        P("segment", "expert", None, "fsdp"),
        P("segment", "expert", None, "fsdp"),
        P("segment", "expert", "fsdp", None),
    )
    out_specs = (
        P("segment", None, ("expert", "fsdp"), None),
        P("segment", None, ("expert", "fsdp"), None),
        P("segment", "expert", None, "fsdp"),
        P("segment", "expert", None, "fsdp"),
        P("segment", "expert", "fsdp", None),
    )
    return jax.shard_map(relay, mesh=mesh, in_specs=in_specs, out_specs=out_specs, check_vma=False)
```

```python
import functools

import jax
import jax.numpy as jnp
from jax import lax
from jax.experimental import pallas as pl
from jax.experimental.pallas import tpu as pltpu
from jax.sharding import PartitionSpec as P

MESH = pl.DeviceIdType.MESH
LANES = 128
ROWS = 16
TILE = 256
GRANT = 62 << 20
ROOM = 44 << 20
PARTS = 2
CONTRACT_COLS = (((1,), (1,)), ((), ()))


def relay_kernel(
    segments, n_expert, n_fsdp,
    acts, out_grad, ids, gates, w_gate, w_up, w_down,
    act_out, gate_out, xt_out, g_out, da_out, db_out, hgt_out,
    wg, wu, wd, xbuf, gbuf, rbuf, zbuf, rst, zst, newg,
    slope_buf, act_buf, hid_buf, qbuf, da, db, hg, xt, hgt,
    in_sem, out_sem, go, xs, xr, os, gr, ds, rs, rr, zs, zr,
):
    group = n_expert * n_fsdp
    micros, toks, width = acts.shape[1:]
    hid = wg.shape[1]
    rows = group * toks
    last = segments - 1
    part_width = newg.shape[2]
    parts = width // part_width
    seg = lax.axis_index("segment")
    expert = lax.axis_index("expert")
    fsdp = lax.axis_index("fsdp")
    me = expert * n_fsdp + fsdp
    is_last = seg == last
    tiles = [(s, min(TILE, hid - s)) for s in range(0, hid, TILE)]
    d_tiles = [(s, min(TILE, part_width - s)) for s in range(0, part_width, TILE)]

    def at(layer, member):
        return (layer, member // n_fsdp, member % n_fsdp)

    def turn_round(first, count, start, fn):
        def body(i, carry):
            fn((start + i) % count)
            return carry
        lax.fori_loop(first, count, body, 0)

    def others(fn):
        turn_round(1, group, me, fn)

    def members(fn):
        turn_round(0, group, me, fn)

    def other_experts(fn):
        turn_round(1, n_expert, expert, fn)

    def other_fsdp(fn):
        turn_round(1, n_fsdp, fsdp, fn)

    def own_loss(m, c):
        return pltpu.make_async_copy(
            out_grad.at[m, :, pl.ds(c * part_width, part_width)], gbuf.at[m * parts + c, me],
            in_sem.at[3 + micros + m * parts + c])

    own_acts = [
        pltpu.make_async_copy(acts.at[0, m], xbuf.at[m, me, :, pl.ds(0, width)], in_sem.at[3 + m])
        for m in range(micros)
    ]
    for copy in own_acts:
        copy.start()

    @pl.when(is_last)
    def _():
        for m in range(micros):
            for c in range(parts):
                own_loss(m, c).start()

    loads = [
        pltpu.make_async_copy(src.at[0, 0], dst, in_sem.at[i])
        for i, (src, dst) in enumerate(((w_gate, wg), (w_up, wu), (w_down, wd)))
    ]
    for load in loads:
        load.start()

    barrier = pltpu.get_barrier_semaphore()

    def greet(layer):
        def tell(j):
            pl.semaphore_signal(barrier, inc=1, device_id=at(layer, j), device_id_type=MESH)
        return tell

    others(greet(seg))

    @pl.when(seg > 0)
    def _():
        members(greet(seg - 1))

    @pl.when(seg < last)
    def _():
        members(greet(seg + 1))

    lane = lax.broadcasted_iota(jnp.int32, (toks, LANES), 1)
    for m in range(micros):
        named = ids[0, m].T
        weight = gates[0, m].astype(jnp.float32).T
        spread = jnp.zeros((toks, LANES), jnp.float32)
        for k in range(named.shape[1]):
            spread = spread + jnp.where(named[:, k : k + 1] == lane, weight[:, k : k + 1], 0.0)
        xbuf[m, me, :, width:] = spread.astype(jnp.bfloat16)

    below, above = (seg + last) // segments, (2 * last - seg) // segments
    pl.semaphore_wait(barrier, group - 1 + group * below + group * above)

    def x_copy(p, block, j, slot):
        return pltpu.make_async_remote_copy(
            xbuf.at[p, block], xbuf.at[p, block], xs.at[p, slot], xr.at[p, block],
            device_id=at(seg, j), device_id_type=MESH)

    def own_copy(p, block, j, slot):
        return pltpu.make_async_remote_copy(
            gbuf.at[p, block], gbuf.at[p, block], os.at[p, slot], gr.at[p, block],
            device_id=at(seg, j), device_id_type=MESH)

    def down_copy(p, block, j):
        return pltpu.make_async_remote_copy(
            newg.at[p], gbuf.at[p, block], ds.at[p, j], gr.at[p, block],
            device_id=at(lax.max(seg - 1, 0), j), device_id_type=MESH)

    def r_copy(p, block, j):
        return pltpu.make_async_remote_copy(
            rst.at[p, j], rbuf.at[p, block], rs.at[p, j], rr.at[p, block],
            device_id=at(seg, j), device_id_type=MESH)

    def z_copy(block, j):
        return pltpu.make_async_remote_copy(
            zst.at[j], zbuf.at[block], zs.at[j], zr.at[block],
            device_id=at(seg, j), device_id_type=MESH)

    def spread_own(copy, p):
        def along(e):
            j = e * n_fsdp + fsdp
            copy(p, me, j, j).start()

        def across(f):
            j = expert * n_fsdp + f
            copy(p, me, j, j).start()

        other_experts(along)
        other_fsdp(across)

    def pass_on(copy, p):
        def along(e):
            block = e * n_fsdp + fsdp
            copy(p, block, block, block).wait_recv()

            def across(f):
                copy(p, block, expert * n_fsdp + f, e * n_fsdp + f).start()

            other_fsdp(across)

        other_experts(along)

    def take_rest(copy, p):
        def across(f):
            def along(e, carry):
                block = e * n_fsdp + f
                copy(p, block, block, block).wait_recv()
                return carry
            lax.fori_loop(0, n_expert, along, 0)
        other_fsdp(across)

    def spread_sent(copy, p):
        others(lambda j: copy(p, me, j, j).wait_send())

    def pieces(m):
        return range(m * parts, (m + 1) * parts)

    def send_loss(m):
        for c in range(parts):
            own_loss(m, c).wait()
        for p in pieces(m):
            spread_own(own_copy, p)

    def pass_loss(m):
        for p in pieces(m):
            pass_on(own_copy, p)

    def allow_next():
        @pl.when(seg > 0)
        def _():
            pl.semaphore_signal(go, inc=1, device_id=at(seg - 1, me), device_id_type=MESH)

    for copy in own_acts:
        copy.wait()

    @pl.when(is_last)
    def _():
        for m in range(micros):
            spread_own(x_copy, m)
            send_loss(m)
        pass_on(x_copy, 0)
        pass_loss(0)
        take_rest(x_copy, 0)
        allow_next()

    @pl.when(seg < last)
    def _():
        pl.semaphore_wait(go, 1)
        for m in range(micros):
            spread_own(x_copy, m)
        for m in range(micros):
            pass_on(x_copy, m)
        for m in range(micros):
            take_rest(x_copy, m)
        allow_next()

    stores = []

    def keep(src, dst):
        copy = pltpu.make_async_copy(src, dst, out_sem.at[len(stores)])
        copy.start()
        stores.append(copy)

    def prepare(m):
        x = xbuf[m, :, :, :width].reshape(rows, width)
        weights = xbuf[m, :, :, width:].reshape(rows, LANES).astype(jnp.float32)
        mine = lax.broadcasted_iota(jnp.int32, (rows, LANES), 1) == expert
        c = jnp.sum(jnp.where(mine, weights, 0.0), axis=1, keepdims=True)
        for s, size in tiles:
            cut = slice(s, s + size)
            a = jnp.dot(x, wg[:, cut], preferred_element_type=jnp.float32)
            b = jnp.dot(x, wu[:, cut], preferred_element_type=jnp.float32)
            sigmoid = jax.nn.sigmoid(a)
            silu = a * sigmoid
            hidden = silu * b
            slope_buf[m, :, cut] = c * b * (sigmoid * (1.0 + a * (1.0 - sigmoid)))
            act_buf[m, :, cut] = c * silu
            hid_buf[m, :, cut] = hidden
            hg[m, :, cut] = (hidden * c).astype(jnp.bfloat16)

    def transpose(m):
        cut = slice(m * rows, (m + 1) * rows)
        xt[:, cut] = xbuf[m, :, :, :width].reshape(rows, width).T
        hgt[:, cut] = hg[m].T

    def partial(m):
        z = jnp.zeros((rows, 1), jnp.float32)
        for c, p in enumerate(pieces(m)):
            @pl.when(is_last)
            def _():
                take_rest(own_copy, p)

            @pl.when(seg < last)
            def _():
                members(lambda j: own_copy(p, j, j, j).wait_recv())

            g = gbuf[p].reshape(rows, part_width)
            columns = slice(c * part_width, (c + 1) * part_width)
            for s, size in tiles:
                cut = slice(s, s + size)
                q = lax.dot_general(
                    g, wd[cut, columns], CONTRACT_COLS, preferred_element_type=jnp.float32)
                if c > 0:
                    q = q + qbuf[:, cut]
                if c < parts - 1:
                    qbuf[:, cut] = q
                else:
                    da[m, :, cut] = (q * slope_buf[m, :, cut]).astype(jnp.bfloat16)
                    db[m, :, cut] = (q * act_buf[m, :, cut]).astype(jnp.bfloat16)
                    z = z + jnp.sum(q * hid_buf[m, :, cut], axis=1, keepdims=True)
        for c, p in enumerate(pieces(m)):
            for s, size in d_tiles:
                cut = slice(c * part_width + s, c * part_width + s + size)
                r = lax.dot_general(
                    da[m], wg[cut, :], CONTRACT_COLS, preferred_element_type=jnp.float32)
                r = r + lax.dot_general(
                    db[m], wu[cut, :], CONTRACT_COLS, preferred_element_type=jnp.float32)
                rst[p, :, :, s : s + size] = r.astype(jnp.bfloat16).reshape(group, toks, size)
            others(lambda j: r_copy(p, me, j).start())
            rbuf[p, me] = rst[p, me]
        zst[:, m] = jnp.broadcast_to(z, (rows, LANES)).astype(jnp.bfloat16).reshape(group, toks, LANES)

    def combine(m):
        for c, p in enumerate(pieces(m)):
            others(lambda j: r_copy(p, j, j).wait_recv())
            total = gbuf[p, me].astype(jnp.float32)
            for e in range(n_expert):
                part = rbuf[p, e * n_fsdp].astype(jnp.float32)
                for f in range(1, n_fsdp):
                    part = part + rbuf[p, e * n_fsdp + f].astype(jnp.float32)
                total = total + part.astype(jnp.bfloat16).astype(jnp.float32)
            fresh = total.astype(jnp.bfloat16)
            newg[p] = fresh

            @pl.when(seg > 0)
            def _():
                members(lambda j: down_copy(p, me, j).start())

            act_out[0, m, :, c * part_width : (c + 1) * part_width] = fresh

    for load in loads:
        load.wait()
    prepare(0)

    @pl.when(is_last)
    def _():
        for m in range(1, micros):
            pass_on(x_copy, m)
            pass_loss(m)

    @pl.when(seg < last)
    def _():
        for m in range(1, micros):
            prepare(m)

    @pl.when(seg == 0)
    def _():
        for m in range(micros):
            if segments > 1:
                transpose(m)

    for m in range(micros):
        if m > 0:
            @pl.when(is_last)
            def _():
                take_rest(x_copy, m)
                prepare(m)
        partial(m)

    zbuf[me] = zst[me]
    others(lambda j: z_copy(me, j).start())
    for m in range(micros):
        for c, p in enumerate(pieces(m)):
            keep(gbuf.at[p], g_out.at[m, :, :, pl.ds(c * part_width, part_width)])
        keep(da.at[m], da_out.at[m])
        keep(db.at[m], db_out.at[m])
    turned = [
        pltpu.make_async_copy(src, dst, out_sem.at[len(stores) + i])
        for i, (src, dst) in enumerate(((xt, xt_out), (hgt, hgt_out)))
    ]
    early = seg + (segments == 1) == 0
    late = seg + (segments == 1) > 0

    @pl.when(early)
    def _():
        for copy in turned:
            copy.start()

    for m in range(micros):
        combine(m)

    @pl.when(late)
    def _():
        for m in range(micros):
            transpose(m)
        for copy in turned:
            copy.start()

    others(lambda j: z_copy(j, j).wait_recv())
    for m in range(micros):
        named = ids[0, m].T
        total = jnp.zeros(named.shape, jnp.float32)
        for e in range(n_expert):
            part = zbuf[e * n_fsdp, m].astype(jnp.float32)
            for f in range(1, n_fsdp):
                part = part + zbuf[e * n_fsdp + f, m].astype(jnp.float32)
            part = part.astype(jnp.bfloat16).astype(jnp.float32)
            total = total + jnp.where(named == e, part[:, : named.shape[1]], 0.0)
        gate_out[0, m] = total.T

    for m in range(micros):
        spread_sent(x_copy, m)
        for p in pieces(m):
            others(lambda j: r_copy(p, me, j).wait_send())

            @pl.when(is_last)
            def _():
                spread_sent(own_copy, p)

            @pl.when(seg > 0)
            def _():
                members(lambda j: down_copy(p, me, j).wait_send())
    others(lambda j: z_copy(me, j).wait_send())
    for copy in stores + turned:
        copy.wait()


def weight_kernel(
    xt, da, db, hgt, g, act, gate, grad_gate, grad_up, grad_down, act_out, gate_out,
    xt_v, da_v, db_v, hgt_v, g_v, made, in_sem, out_sem,
):
    loads = [
        pltpu.make_async_copy(src, dst, in_sem.at[i])
        for i, (src, dst) in enumerate(((xt, xt_v), (da, da_v), (db, db_v), (hgt, hgt_v), (g, g_v)))
    ]
    for load in loads:
        load.start()
    stores = [
        pltpu.make_async_copy(src, dst, out_sem.at[i])
        for i, (src, dst) in enumerate(((act, act_out), (gate, gate_out)))
    ]
    for copy in stores:
        copy.start()
    products = (
        (xt_v, da_v, grad_gate, loads[:2]),
        (xt_v, db_v, grad_up, loads[2:3]),
        (hgt_v, g_v, grad_down, loads[3:]),
    )
    base = 0
    for left, right, result, needed in products:
        for load in needed:
            load.wait()
        height, columns = left.shape[0], right.shape[1]
        for s in range(0, height, TILE):
            size = min(TILE, height - s)
            tile = jnp.dot(left[s : s + size, :], right[...], preferred_element_type=jnp.float32)
            place = made.at[pl.ds(base + s, size), pl.ds(0, columns)]
            place[...] = tile.astype(jnp.bfloat16)
            copy = pltpu.make_async_copy(
                place, result.at[0, 0, pl.ds(s, size)], out_sem.at[len(stores)])
            copy.start()
            stores.append(copy)
        base += height
    for copy in stores:
        copy.wait()


def weight_grads(xt, da, db, hgt, g, act, gate):
    width, rows = xt.shape
    hid = da.shape[1]
    bf16 = jnp.bfloat16
    far = pl.BlockSpec(memory_space=pl.ANY)
    stores = 2 + 2 * -(-width // TILE) + -(-hid // TILE)
    return pl.pallas_call(
        weight_kernel,
        out_shape=(
            jax.ShapeDtypeStruct((1, 1, width, hid), bf16),
            jax.ShapeDtypeStruct((1, 1, width, hid), bf16),
            jax.ShapeDtypeStruct((1, 1, hid, width), bf16),
            jax.ShapeDtypeStruct(act.shape, act.dtype),
            jax.ShapeDtypeStruct(gate.shape, gate.dtype),
        ),
        in_specs=[far] * 7,
        out_specs=(far,) * 5,
        scratch_shapes=[
            pltpu.VMEM((width, rows), bf16),
            pltpu.VMEM((rows, hid), bf16),
            pltpu.VMEM((rows, hid), bf16),
            pltpu.VMEM((hid, rows), bf16),
            pltpu.VMEM((rows, width), bf16),
            pltpu.VMEM((2 * width + hid, max(width, hid)), bf16),
            pltpu.SemaphoreType.DMA((5,)),
            pltpu.SemaphoreType.DMA((stores,)),
        ],
        compiler_params=pltpu.CompilerParams(vmem_limit_bytes=GRANT),
        cost_estimate=pl.CostEstimate(
            flops=6 * rows * width * hid, bytes_accessed=6 * width * hid, transcendentals=0
        ),
    )(xt, da, db, hgt, g, act, gate)


def relay_room(acts, w_gate, group):
    micros, toks, width = acts.shape[1:]
    hid = w_gate.shape[3]
    rows = micros * group * toks
    return 3 * width * hid * 2 + rows * (width * 2 * 4 + hid * (4 * 4 + 4 * 2) + width * 2 + LANES * 6)


def relay(acts, out_grad, ids, gates, w_gate, w_up, w_down):
    segments = lax.axis_size("segment")
    n_expert = lax.axis_size("expert")
    n_fsdp = lax.axis_size("fsdp")
    group = n_expert * n_fsdp
    micros, toks, width = acts.shape[1:]
    hid = w_gate.shape[3]
    fits = (
        toks % ROWS == 0
        and group * toks % LANES == 0
        and width % LANES == 0
        and hid % LANES == 0
        and n_expert <= LANES
        and relay_room(acts, w_gate, group) <= ROOM
    )
    if not fits:
        return local(acts, out_grad, ids, gates, w_gate, w_up, w_down)
    rows = group * toks
    parts = PARTS if width % (PARTS * LANES) == 0 else 1
    pieces = micros * parts
    piece = (pieces, group, toks, width // parts)
    bf16, f32 = jnp.bfloat16, jnp.float32
    vmem = pl.BlockSpec(memory_space=pltpu.VMEM)
    far = pl.BlockSpec(memory_space=pl.ANY)
    home = pl.BlockSpec(memory_space=pltpu.HBM)
    dma = pltpu.SemaphoreType.DMA
    scratch = [
        pltpu.VMEM((width, hid), bf16),
        pltpu.VMEM((width, hid), bf16),
        pltpu.VMEM((hid, width), bf16),
        pltpu.VMEM((micros, group, toks, width + LANES), bf16),
        pltpu.VMEM(piece, bf16),
        pltpu.VMEM(piece, bf16),
        pltpu.VMEM((group, micros, toks, LANES), bf16),
        pltpu.VMEM(piece, bf16),
        pltpu.VMEM((group, micros, toks, LANES), bf16),
        pltpu.VMEM((pieces, toks, width // parts), bf16),
    ]
    scratch += [pltpu.VMEM((micros, rows, hid), f32)] * 3
    scratch += [pltpu.VMEM((rows, hid), f32)]
    scratch += [pltpu.VMEM((micros, rows, hid), bf16)] * 3
    scratch += [pltpu.VMEM((width, micros * rows), bf16), pltpu.VMEM((hid, micros * rows), bf16)]
    scratch += [dma((3 + micros + pieces,)), dma((2 + 2 * micros + pieces,))]
    scratch += [pltpu.SemaphoreType.REGULAR]
    scratch += [dma((micros, group))] * 2
    scratch += [dma((pieces, group))] * 5
    scratch += [dma((group,))] * 2
    flops = 2 * micros * rows * width * hid * 5
    outs = pl.pallas_call(
        functools.partial(relay_kernel, segments, n_expert, n_fsdp),
        out_shape=(
            jax.ShapeDtypeStruct(acts.shape, bf16),
            jax.ShapeDtypeStruct(gates.shape[:2] + (gates.shape[3], toks), f32),
            jax.ShapeDtypeStruct((width, micros * rows), bf16),
            jax.ShapeDtypeStruct((micros, group, toks, width), bf16),
            jax.ShapeDtypeStruct((micros, rows, hid), bf16),
            jax.ShapeDtypeStruct((micros, rows, hid), bf16),
            jax.ShapeDtypeStruct((hid, micros * rows), bf16),
        ),
        in_specs=[home, home, vmem, vmem, far, far, far],
        out_specs=(vmem, vmem, far, far, far, far, far),
        scratch_shapes=scratch,
        compiler_params=pltpu.CompilerParams(
            collective_id=0, has_side_effects=True, vmem_limit_bytes=GRANT
        ),
        cost_estimate=pl.CostEstimate(
            flops=flops, bytes_accessed=6 * width * hid, transcendentals=micros * rows * hid
        ),
    )(acts, out_grad, ids.swapaxes(2, 3), gates.swapaxes(2, 3), w_gate, w_up, w_down)
    act_grad, gate_grad, xt, g, da, db, hgt = outs

    grad_gate, grad_up, grad_down, act_grad, gate_grad = weight_grads(
        xt, da.reshape(-1, hid), db.reshape(-1, hid), hgt, g.reshape(-1, width), act_grad, gate_grad)
    return act_grad, gate_grad.swapaxes(2, 3), grad_gate, grad_up, grad_down


def from_behind(value, axis, steps):
    count = lax.axis_size(axis)
    leading, last = (max(0, -steps), min(count, count - steps))
    return lax.ppermute(value, axis, [(source, source + steps) for source in range(leading, last)])


def silu_parts(pre_gate):
    sigmoid = jax.nn.sigmoid(pre_gate)
    return (pre_gate * sigmoid, sigmoid * (1.0 + pre_gate * (1.0 - sigmoid)))


def local(acts, out_grad, expert_ids, gates, w_gate, w_up, w_down):
    segments = lax.axis_size("segment")
    segment_now = lax.axis_index("segment")
    n_expert = lax.axis_size("expert")
    n_fsdp = lax.axis_size("fsdp")
    micro_count = acts.shape[1]
    tok_count = acts.shape[2]
    width = acts.shape[3]
    top_count = expert_ids.shape[3]
    capacity = 5 * top_count * tok_count // (4 * n_expert)
    w_first = w_gate[0, 0]
    w_third = w_up[0, 0]
    w_second = w_down[0, 0]
    hid_local = w_first.shape[1]
    expert_iota = jnp.arange(n_expert, dtype=jnp.int32)
    slot_iota = jnp.arange(capacity, dtype=jnp.int32)
    micro_iota = jnp.arange(micro_count, dtype=jnp.int32)
    contract_rows = (((0,), (0,)), ((), ()))
    contract_cols = (((1,), (1,)), ((), ()))
    grad_first = jnp.zeros((width, hid_local), jnp.float32)
    grad_third = jnp.zeros((width, hid_local), jnp.float32)
    grad_second = jnp.zeros((hid_local, width), jnp.float32)
    act_out = jnp.zeros(acts.shape, jnp.bfloat16)
    gate_out = jnp.zeros(gates.shape, jnp.float32)
    previous = jnp.zeros((tok_count, width), jnp.bfloat16)
    for moment in range(micro_count + segments - 1):
        micro_index = moment - (segments - 1 - segment_now)
        valid = (micro_index >= 0) & (micro_index < micro_count)
        picked = jnp.clip(micro_index, 0, micro_count - 1)
        tokens_now = lax.dynamic_index_in_dim(acts[0], picked, 0, keepdims=False)
        loss_grad = lax.dynamic_index_in_dim(out_grad, picked, 0, keepdims=False)
        ids_now = lax.dynamic_index_in_dim(expert_ids[0], picked, 0, keepdims=False)
        gates_now = lax.dynamic_index_in_dim(gates[0], picked, 0, keepdims=False)
        if moment > 0:
            incoming = from_behind(previous, "segment", -1)
        else:
            incoming = previous
        grad_now = jnp.where(segment_now == segments - 1, loss_grad, incoming)
        table = (ids_now[:, :, None] == expert_iota).astype(jnp.int32)
        counts = jnp.sum(table, axis=1)
        before = jnp.cumsum(counts, axis=0) - counts
        slots = jnp.sum(before[:, None, :] * table, axis=2)
        routing = (
            (ids_now[None, None] == expert_iota[:, None, None, None])
            & (slots[None, None] == slot_iota[None, :, None, None])
        ).astype(jnp.float32)
        placing = jnp.sum(routing, axis=3).astype(jnp.bfloat16)
        token_buf = jnp.einsum(
            "ect,td->ecd", placing, tokens_now, preferred_element_type=jnp.float32
        ).astype(jnp.bfloat16)
        grad_buf = jnp.einsum(
            "ect,td->ecd", placing, grad_now, preferred_element_type=jnp.float32
        ).astype(jnp.bfloat16)
        gate_buf = jnp.einsum("ectk,tk->ec", routing, gates_now.astype(jnp.float32)).astype(
            jnp.bfloat16
        )
        start_state = (
            grad_first,
            grad_third,
            grad_second,
            jnp.zeros((n_fsdp, n_expert, capacity, width), jnp.bfloat16),
            jnp.zeros((n_fsdp, n_expert, capacity), jnp.bfloat16),
        )
        grouped = (
            lax.all_gather(token_buf[None], "fsdp", axis=0, tiled=True),
            lax.all_gather(grad_buf[None], "fsdp", axis=0, tiled=True),
            lax.all_gather(gate_buf[None], "fsdp", axis=0, tiled=True),
        )
        token_rows = lax.all_to_all(grouped[0], "expert", split_axis=1, concat_axis=1, tiled=True)
        grad_rows = lax.all_to_all(grouped[1], "expert", split_axis=1, concat_axis=1, tiled=True)
        gate_rows = lax.all_to_all(grouped[2], "expert", split_axis=1, concat_axis=1, tiled=True)

        def compute(state):
            sum_first, sum_third, sum_second, part_rows, part_gates = state
            flat_tokens = token_rows.reshape(-1, width)
            flat_grads = grad_rows.reshape(-1, width)
            gate_col = gate_rows.reshape(-1).astype(jnp.float32)[:, None]
            pre_gate = jnp.dot(flat_tokens, w_first, preferred_element_type=jnp.float32)
            pre_up = jnp.dot(flat_tokens, w_third, preferred_element_type=jnp.float32)
            activated, slope_term = silu_parts(pre_gate)
            hidden = activated * pre_up
            back_hidden = lax.dot_general(
                flat_grads, w_second, contract_cols, preferred_element_type=jnp.float32
            )
            scaled = back_hidden * gate_col
            grad_gate_pre = (scaled * pre_up * slope_term).astype(jnp.bfloat16)
            grad_up_pre = (scaled * activated).astype(jnp.bfloat16)
            hidden_gated = (hidden * gate_col).astype(jnp.bfloat16)
            sum_first = sum_first + lax.dot_general(
                flat_tokens, grad_gate_pre, contract_rows, preferred_element_type=jnp.float32
            )
            sum_third = sum_third + lax.dot_general(
                flat_tokens, grad_up_pre, contract_rows, preferred_element_type=jnp.float32
            )
            sum_second = sum_second + lax.dot_general(
                hidden_gated, flat_grads, contract_rows, preferred_element_type=jnp.float32
            )
            partial_value = lax.dot_general(
                grad_gate_pre, w_first, contract_cols, preferred_element_type=jnp.float32
            )
            partial_value = partial_value + lax.dot_general(
                grad_up_pre, w_third, contract_cols, preferred_element_type=jnp.float32
            )
            gate_part = jnp.sum(hidden * back_hidden, axis=1)
            part_rows = partial_value.astype(jnp.bfloat16).reshape(token_rows.shape)
            part_gates = gate_part.astype(jnp.bfloat16).reshape(gate_rows.shape)
            return (sum_first, sum_third, sum_second, part_rows, part_gates)

        finished = lax.cond(valid, compute, lambda state: state, start_state)
        grad_first, grad_third, grad_second, part_rows, part_gates = finished
        summed_rows, summed_gates = (
            lax.psum_scatter(part_rows, "fsdp", scatter_dimension=0, tiled=True).astype(
                jnp.float32
            ),
            lax.psum_scatter(part_gates, "fsdp", scatter_dimension=0, tiled=True).astype(
                jnp.float32
            ),
        )
        back_rows, back_gates = (
            lax.all_to_all(
                summed_rows[0].astype(jnp.bfloat16),
                "expert",
                split_axis=0,
                concat_axis=0,
                tiled=True,
            ),
            lax.all_to_all(
                summed_gates[0].astype(jnp.bfloat16),
                "expert",
                split_axis=0,
                concat_axis=0,
                tiled=True,
            ),
        )
        token_back = jnp.einsum(
            "ect,ecd->td", placing, back_rows, preferred_element_type=jnp.float32
        )
        new_grad = (grad_now.astype(jnp.float32) + token_back).astype(jnp.bfloat16)
        gate_new = jnp.einsum("ectk,ec->tk", routing, back_gates.astype(jnp.float32))
        chosen = micro_iota == micro_index
        act_out = jnp.where(chosen[None, :, None, None], new_grad[None, None], act_out)
        gate_out = jnp.where(chosen[None, :, None, None], gate_new[None, None], gate_out)
        previous = new_grad
    return (
        act_out,
        gate_out,
        grad_first.astype(jnp.bfloat16)[None, None],
        grad_third.astype(jnp.bfloat16)[None, None],
        grad_second.astype(jnp.bfloat16)[None, None],
    )


def solution(mesh):
    in_specs = (
        P("segment", None, ("expert", "fsdp"), None),
        P(None, ("expert", "fsdp"), None),
        P("segment", None, ("expert", "fsdp"), None),
        P("segment", None, ("expert", "fsdp"), None),
        P("segment", "expert", None, "fsdp"),
        P("segment", "expert", None, "fsdp"),
        P("segment", "expert", "fsdp", None),
    )
    out_specs = (
        P("segment", None, ("expert", "fsdp"), None),
        P("segment", None, ("expert", "fsdp"), None),
        P("segment", "expert", None, "fsdp"),
        P("segment", "expert", None, "fsdp"),
        P("segment", "expert", "fsdp", None),
    )
    return jax.shard_map(relay, mesh=mesh, in_specs=in_specs, out_specs=out_specs, check_vma=False)
```

```python
import functools

import jax
import jax.numpy as jnp
from jax import lax
from jax.experimental import pallas as pl
from jax.experimental.pallas import tpu as pltpu
from jax.sharding import PartitionSpec as P

MESH = pl.DeviceIdType.MESH
LANES = 128
ROWS = 16
TILE = 256
GRANT = 62 << 20
ROOM = 44 << 20
PARTS = 2
CONTRACT_COLS = (((1,), (1,)), ((), ()))


def relay_kernel(
    segments, n_expert, n_fsdp,
    acts, out_grad, ids, gates, w_gate, w_up, w_down,
    act_out, gate_out, xt_out, g_out, da_out, db_out, hgt_out,
    wg, wu, wd, xbuf, gbuf, rbuf, zbuf, rst, zst, newg,
    slope_buf, act_buf, hid_buf, qbuf, da, db, hg, xt, hgt, wgt, wut, wdt,
    in_sem, out_sem, go, xs, xr, os, gr, ds, rs, rr, zs, zr,
):
    group = n_expert * n_fsdp
    micros, toks, width = acts.shape[1:]
    hid = wg.shape[1]
    rows = group * toks
    last = segments - 1
    part_width = newg.shape[2]
    parts = width // part_width
    seg = lax.axis_index("segment")
    expert = lax.axis_index("expert")
    fsdp = lax.axis_index("fsdp")
    me = expert * n_fsdp + fsdp
    is_last = seg == last
    tiles = [(s, min(TILE, hid - s)) for s in range(0, hid, TILE)]
    d_tiles = [(s, min(TILE, part_width - s)) for s in range(0, part_width, TILE)]

    def at(layer, member):
        return (layer, member // n_fsdp, member % n_fsdp)

    def turn_round(first, count, start, fn):
        def body(i, carry):
            fn((start + i) % count)
            return carry
        lax.fori_loop(first, count, body, 0)

    def others(fn):
        turn_round(1, group, me, fn)

    def members(fn):
        turn_round(0, group, me, fn)

    def other_experts(fn):
        turn_round(1, n_expert, expert, fn)

    def other_fsdp(fn):
        turn_round(1, n_fsdp, fsdp, fn)

    def own_loss(m, c):
        return pltpu.make_async_copy(
            out_grad.at[m, :, pl.ds(c * part_width, part_width)], gbuf.at[m * parts + c, me],
            in_sem.at[3 + micros + m * parts + c])

    own_acts = [
        pltpu.make_async_copy(acts.at[0, m], xbuf.at[m, me, :, pl.ds(0, width)], in_sem.at[3 + m])
        for m in range(micros)
    ]
    for copy in own_acts:
        copy.start()

    @pl.when(is_last)
    def _():
        for m in range(micros):
            for c in range(parts):
                own_loss(m, c).start()

    loads = [
        pltpu.make_async_copy(src.at[0, 0], dst, in_sem.at[i])
        for i, (src, dst) in enumerate(((w_gate, wg), (w_up, wu), (w_down, wd)))
    ]
    for load in loads:
        load.start()

    barrier = pltpu.get_barrier_semaphore()

    def greet(layer):
        def tell(j):
            pl.semaphore_signal(barrier, inc=1, device_id=at(layer, j), device_id_type=MESH)
        return tell

    others(greet(seg))

    @pl.when(seg > 0)
    def _():
        members(greet(seg - 1))

    @pl.when(seg < last)
    def _():
        members(greet(seg + 1))

    lane = lax.broadcasted_iota(jnp.int32, (toks, LANES), 1)
    for m in range(micros):
        named = ids[0, m].T
        weight = gates[0, m].astype(jnp.float32).T
        spread = jnp.zeros((toks, LANES), jnp.float32)
        for k in range(named.shape[1]):
            spread = spread + jnp.where(named[:, k : k + 1] == lane, weight[:, k : k + 1], 0.0)
        xbuf[m, me, :, width:] = spread.astype(jnp.bfloat16)

    below, above = (seg + last) // segments, (2 * last - seg) // segments
    pl.semaphore_wait(barrier, group - 1 + group * below + group * above)

    def x_copy(p, block, j, slot):
        return pltpu.make_async_remote_copy(
            xbuf.at[p, block], xbuf.at[p, block], xs.at[p, slot], xr.at[p, block],
            device_id=at(seg, j), device_id_type=MESH)

    def own_copy(p, block, j, slot):
        return pltpu.make_async_remote_copy(
            gbuf.at[p, block], gbuf.at[p, block], os.at[p, slot], gr.at[p, block],
            device_id=at(seg, j), device_id_type=MESH)

    def down_copy(p, block, j):
        return pltpu.make_async_remote_copy(
            newg.at[p], gbuf.at[p, block], ds.at[p, j], gr.at[p, block],
            device_id=at(lax.max(seg - 1, 0), j), device_id_type=MESH)

    def r_copy(p, block, j):
        return pltpu.make_async_remote_copy(
            rst.at[p, j], rbuf.at[p, block], rs.at[p, j], rr.at[p, block],
            device_id=at(seg, j), device_id_type=MESH)

    def z_copy(block, j):
        return pltpu.make_async_remote_copy(
            zst.at[j], zbuf.at[block], zs.at[j], zr.at[block],
            device_id=at(seg, j), device_id_type=MESH)

    def spread_own(copy, p):
        def along(e):
            j = e * n_fsdp + fsdp
            copy(p, me, j, j).start()

        def across(f):
            j = expert * n_fsdp + f
            copy(p, me, j, j).start()

        other_experts(along)
        other_fsdp(across)

    def pass_on(copy, p):
        def along(e):
            block = e * n_fsdp + fsdp
            copy(p, block, block, block).wait_recv()

            def across(f):
                copy(p, block, expert * n_fsdp + f, e * n_fsdp + f).start()

            other_fsdp(across)

        other_experts(along)

    def take_rest(copy, p):
        def across(f):
            def along(e, carry):
                block = e * n_fsdp + f
                copy(p, block, block, block).wait_recv()
                return carry
            lax.fori_loop(0, n_expert, along, 0)
        other_fsdp(across)

    def spread_sent(copy, p):
        others(lambda j: copy(p, me, j, j).wait_send())

    def pieces(m):
        return range(m * parts, (m + 1) * parts)

    def send_loss(m):
        for c in range(parts):
            own_loss(m, c).wait()
        for p in pieces(m):
            spread_own(own_copy, p)

    def pass_loss(m):
        for p in pieces(m):
            pass_on(own_copy, p)

    def allow_next():
        @pl.when(seg > 0)
        def _():
            pl.semaphore_signal(go, inc=1, device_id=at(seg - 1, me), device_id_type=MESH)

    for copy in own_acts:
        copy.wait()

    @pl.when(is_last)
    def _():
        for m in range(micros):
            spread_own(x_copy, m)
            send_loss(m)
        pass_on(x_copy, 0)
        pass_loss(0)
        take_rest(x_copy, 0)
        allow_next()

    for load in loads:
        load.wait()

    @pl.when(seg < last)
    def _():
        for src, dst in ((wg, wgt), (wu, wut), (wd, wdt)):
            for s in range(0, src.shape[0], TILE):
                e = min(s + TILE, src.shape[0])
                dst[:, s:e] = src[s:e, :].T
        pl.semaphore_wait(go, 1)
        for m in range(micros):
            spread_own(x_copy, m)
        for m in range(micros):
            pass_on(x_copy, m)
        for m in range(micros):
            take_rest(x_copy, m)
        allow_next()

    stores = []

    def keep(src, dst):
        copy = pltpu.make_async_copy(src, dst, out_sem.at[len(stores)])
        copy.start()
        stores.append(copy)

    def prepare(m):
        x = xbuf[m, :, :, :width].reshape(rows, width)
        weights = xbuf[m, :, :, width:].reshape(rows, LANES).astype(jnp.float32)
        mine = lax.broadcasted_iota(jnp.int32, (rows, LANES), 1) == expert
        c = jnp.sum(jnp.where(mine, weights, 0.0), axis=1, keepdims=True)
        for s, size in tiles:
            cut = slice(s, s + size)
            a = jnp.dot(x, wg[:, cut], preferred_element_type=jnp.float32)
            b = jnp.dot(x, wu[:, cut], preferred_element_type=jnp.float32)
            sigmoid = jax.nn.sigmoid(a)
            silu = a * sigmoid
            hidden = silu * b
            slope_buf[m, :, cut] = c * b * (sigmoid * (1.0 + a * (1.0 - sigmoid)))
            act_buf[m, :, cut] = c * silu
            hid_buf[m, :, cut] = hidden
            hg[m, :, cut] = (hidden * c).astype(jnp.bfloat16)

    def transpose(m):
        cut = slice(m * rows, (m + 1) * rows)
        xt[:, cut] = xbuf[m, :, :, :width].reshape(rows, width).T
        hgt[:, cut] = hg[m].T

    def times(left, kept, turned, cut, along, flat):
        if flat:
            return lax.dot_general(
                left, kept[cut, along], CONTRACT_COLS, preferred_element_type=jnp.float32)
        return jnp.dot(left, turned[along, cut], preferred_element_type=jnp.float32)

    def partial(m, flat):
        z = jnp.zeros((rows, 1), jnp.float32)
        for c, p in enumerate(pieces(m)):
            if flat:
                take_rest(own_copy, p)
            else:
                members(lambda j: own_copy(p, j, j, j).wait_recv())

            g = gbuf[p].reshape(rows, part_width)
            columns = slice(c * part_width, (c + 1) * part_width)
            for s, size in tiles:
                cut = slice(s, s + size)
                q = times(g, wd, wdt, cut, columns, flat)
                if c > 0:
                    q = q + qbuf[:, cut]
                if c < parts - 1:
                    qbuf[:, cut] = q
                else:
                    da[m, :, cut] = (q * slope_buf[m, :, cut]).astype(jnp.bfloat16)
                    db[m, :, cut] = (q * act_buf[m, :, cut]).astype(jnp.bfloat16)
                    z = z + jnp.sum(q * hid_buf[m, :, cut], axis=1, keepdims=True)
        for c, p in enumerate(pieces(m)):
            for s, size in d_tiles:
                cut = slice(c * part_width + s, c * part_width + s + size)
                r = times(da[m], wg, wgt, cut, slice(None), flat)
                r = r + times(db[m], wu, wut, cut, slice(None), flat)
                rst[p, :, :, s : s + size] = r.astype(jnp.bfloat16).reshape(group, toks, size)
            others(lambda j: r_copy(p, me, j).start())
            rbuf[p, me] = rst[p, me]
        zst[:, m] = jnp.broadcast_to(z, (rows, LANES)).astype(jnp.bfloat16).reshape(group, toks, LANES)

    def combine(m):
        for c, p in enumerate(pieces(m)):
            others(lambda j: r_copy(p, j, j).wait_recv())
            total = gbuf[p, me].astype(jnp.float32)
            for e in range(n_expert):
                part = rbuf[p, e * n_fsdp].astype(jnp.float32)
                for f in range(1, n_fsdp):
                    part = part + rbuf[p, e * n_fsdp + f].astype(jnp.float32)
                total = total + part.astype(jnp.bfloat16).astype(jnp.float32)
            fresh = total.astype(jnp.bfloat16)
            newg[p] = fresh

            @pl.when(seg > 0)
            def _():
                members(lambda j: down_copy(p, me, j).start())

            act_out[0, m, :, c * part_width : (c + 1) * part_width] = fresh

    prepare(0)

    @pl.when(is_last)
    def _():
        for m in range(1, micros):
            pass_on(x_copy, m)
            pass_loss(m)

    @pl.when(seg < last)
    def _():
        for m in range(1, micros):
            prepare(m)

    @pl.when(seg == 0)
    def _():
        for m in range(micros):
            if segments > 1:
                transpose(m)

    for m in range(micros):
        if m > 0:
            @pl.when(is_last)
            def _():
                take_rest(x_copy, m)
                prepare(m)

        @pl.when(is_last)
        def _():
            partial(m, True)

        if segments > 1:
            @pl.when(seg < last)
            def _():
                partial(m, False)

    zbuf[me] = zst[me]
    others(lambda j: z_copy(me, j).start())
    for m in range(micros):
        for c, p in enumerate(pieces(m)):
            keep(gbuf.at[p], g_out.at[m, :, :, pl.ds(c * part_width, part_width)])
        keep(da.at[m], da_out.at[m])
        keep(db.at[m], db_out.at[m])
    turned = [
        pltpu.make_async_copy(src, dst, out_sem.at[len(stores) + i])
        for i, (src, dst) in enumerate(((xt, xt_out), (hgt, hgt_out)))
    ]
    early = seg + (segments == 1) == 0
    late = seg + (segments == 1) > 0

    @pl.when(early)
    def _():
        for copy in turned:
            copy.start()

    for m in range(micros):
        combine(m)

    @pl.when(late)
    def _():
        for m in range(micros):
            transpose(m)
        for copy in turned:
            copy.start()

    others(lambda j: z_copy(j, j).wait_recv())
    for m in range(micros):
        named = ids[0, m].T
        total = jnp.zeros(named.shape, jnp.float32)
        for e in range(n_expert):
            part = zbuf[e * n_fsdp, m].astype(jnp.float32)
            for f in range(1, n_fsdp):
                part = part + zbuf[e * n_fsdp + f, m].astype(jnp.float32)
            part = part.astype(jnp.bfloat16).astype(jnp.float32)
            total = total + jnp.where(named == e, part[:, : named.shape[1]], 0.0)
        gate_out[0, m] = total.T

    for m in range(micros):
        spread_sent(x_copy, m)
        for p in pieces(m):
            others(lambda j: r_copy(p, me, j).wait_send())

            @pl.when(is_last)
            def _():
                spread_sent(own_copy, p)

            @pl.when(seg > 0)
            def _():
                members(lambda j: down_copy(p, me, j).wait_send())
    others(lambda j: z_copy(me, j).wait_send())
    for copy in stores + turned:
        copy.wait()


def weight_kernel(
    xt, da, db, hgt, g, act, gate, grad_gate, grad_up, grad_down, act_out, gate_out,
    xt_v, da_v, db_v, hgt_v, g_v, made, in_sem, out_sem,
):
    loads = [
        pltpu.make_async_copy(src, dst, in_sem.at[i])
        for i, (src, dst) in enumerate(((xt, xt_v), (da, da_v), (db, db_v), (hgt, hgt_v), (g, g_v)))
    ]
    for load in loads:
        load.start()
    stores = [
        pltpu.make_async_copy(src, dst, out_sem.at[i])
        for i, (src, dst) in enumerate(((act, act_out), (gate, gate_out)))
    ]
    for copy in stores:
        copy.start()
    products = (
        (xt_v, da_v, grad_gate, loads[:2]),
        (xt_v, db_v, grad_up, loads[2:3]),
        (hgt_v, g_v, grad_down, loads[3:]),
    )
    base = 0
    for left, right, result, needed in products:
        for load in needed:
            load.wait()
        height, columns = left.shape[0], right.shape[1]
        for s in range(0, height, TILE):
            size = min(TILE, height - s)
            tile = jnp.dot(left[s : s + size, :], right[...], preferred_element_type=jnp.float32)
            place = made.at[pl.ds(base + s, size), pl.ds(0, columns)]
            place[...] = tile.astype(jnp.bfloat16)
            copy = pltpu.make_async_copy(
                place, result.at[0, 0, pl.ds(s, size)], out_sem.at[len(stores)])
            copy.start()
            stores.append(copy)
        base += height
    for copy in stores:
        copy.wait()


def weight_grads(xt, da, db, hgt, g, act, gate):
    width, rows = xt.shape
    hid = da.shape[1]
    bf16 = jnp.bfloat16
    far = pl.BlockSpec(memory_space=pl.ANY)
    stores = 2 + 2 * -(-width // TILE) + -(-hid // TILE)
    return pl.pallas_call(
        weight_kernel,
        out_shape=(
            jax.ShapeDtypeStruct((1, 1, width, hid), bf16),
            jax.ShapeDtypeStruct((1, 1, width, hid), bf16),
            jax.ShapeDtypeStruct((1, 1, hid, width), bf16),
            jax.ShapeDtypeStruct(act.shape, act.dtype),
            jax.ShapeDtypeStruct(gate.shape, gate.dtype),
        ),
        in_specs=[far] * 7,
        out_specs=(far,) * 5,
        scratch_shapes=[
            pltpu.VMEM((width, rows), bf16),
            pltpu.VMEM((rows, hid), bf16),
            pltpu.VMEM((rows, hid), bf16),
            pltpu.VMEM((hid, rows), bf16),
            pltpu.VMEM((rows, width), bf16),
            pltpu.VMEM((2 * width + hid, max(width, hid)), bf16),
            pltpu.SemaphoreType.DMA((5,)),
            pltpu.SemaphoreType.DMA((stores,)),
        ],
        compiler_params=pltpu.CompilerParams(vmem_limit_bytes=GRANT),
        cost_estimate=pl.CostEstimate(
            flops=6 * rows * width * hid, bytes_accessed=6 * width * hid, transcendentals=0
        ),
    )(xt, da, db, hgt, g, act, gate)


def relay_room(acts, w_gate, group):
    micros, toks, width = acts.shape[1:]
    hid = w_gate.shape[3]
    rows = micros * group * toks
    return 6 * width * hid * 2 + rows * (width * 2 * 4 + hid * (4 * 4 + 4 * 2) + width * 2 + LANES * 6)


def relay(acts, out_grad, ids, gates, w_gate, w_up, w_down):
    segments = lax.axis_size("segment")
    n_expert = lax.axis_size("expert")
    n_fsdp = lax.axis_size("fsdp")
    group = n_expert * n_fsdp
    micros, toks, width = acts.shape[1:]
    hid = w_gate.shape[3]
    fits = (
        toks % ROWS == 0
        and group * toks % LANES == 0
        and width % LANES == 0
        and hid % LANES == 0
        and n_expert <= LANES
        and relay_room(acts, w_gate, group) <= ROOM
    )
    if not fits:
        return local(acts, out_grad, ids, gates, w_gate, w_up, w_down)
    rows = group * toks
    parts = PARTS if width % (PARTS * LANES) == 0 else 1
    pieces = micros * parts
    piece = (pieces, group, toks, width // parts)
    bf16, f32 = jnp.bfloat16, jnp.float32
    vmem = pl.BlockSpec(memory_space=pltpu.VMEM)
    far = pl.BlockSpec(memory_space=pl.ANY)
    home = pl.BlockSpec(memory_space=pltpu.HBM)
    dma = pltpu.SemaphoreType.DMA
    scratch = [
        pltpu.VMEM((width, hid), bf16),
        pltpu.VMEM((width, hid), bf16),
        pltpu.VMEM((hid, width), bf16),
        pltpu.VMEM((micros, group, toks, width + LANES), bf16),
        pltpu.VMEM(piece, bf16),
        pltpu.VMEM(piece, bf16),
        pltpu.VMEM((group, micros, toks, LANES), bf16),
        pltpu.VMEM(piece, bf16),
        pltpu.VMEM((group, micros, toks, LANES), bf16),
        pltpu.VMEM((pieces, toks, width // parts), bf16),
    ]
    scratch += [pltpu.VMEM((micros, rows, hid), f32)] * 3
    scratch += [pltpu.VMEM((rows, hid), f32)]
    scratch += [pltpu.VMEM((micros, rows, hid), bf16)] * 3
    scratch += [pltpu.VMEM((width, micros * rows), bf16), pltpu.VMEM((hid, micros * rows), bf16)]
    scratch += [pltpu.VMEM((hid, width), bf16)] * 2 + [pltpu.VMEM((width, hid), bf16)]
    scratch += [dma((3 + micros + pieces,)), dma((2 + 2 * micros + pieces,))]
    scratch += [pltpu.SemaphoreType.REGULAR]
    scratch += [dma((micros, group))] * 2
    scratch += [dma((pieces, group))] * 5
    scratch += [dma((group,))] * 2
    flops = 2 * micros * rows * width * hid * 5
    outs = pl.pallas_call(
        functools.partial(relay_kernel, segments, n_expert, n_fsdp),
        out_shape=(
            jax.ShapeDtypeStruct(acts.shape, bf16),
            jax.ShapeDtypeStruct(gates.shape[:2] + (gates.shape[3], toks), f32),
            jax.ShapeDtypeStruct((width, micros * rows), bf16),
            jax.ShapeDtypeStruct((micros, group, toks, width), bf16),
            jax.ShapeDtypeStruct((micros, rows, hid), bf16),
            jax.ShapeDtypeStruct((micros, rows, hid), bf16),
            jax.ShapeDtypeStruct((hid, micros * rows), bf16),
        ),
        in_specs=[home, home, vmem, vmem, far, far, far],
        out_specs=(vmem, vmem, far, far, far, far, far),
        scratch_shapes=scratch,
        compiler_params=pltpu.CompilerParams(
            collective_id=0, has_side_effects=True, vmem_limit_bytes=GRANT
        ),
        cost_estimate=pl.CostEstimate(
            flops=flops, bytes_accessed=6 * width * hid, transcendentals=micros * rows * hid
        ),
    )(acts, out_grad, ids.swapaxes(2, 3), gates.swapaxes(2, 3), w_gate, w_up, w_down)
    act_grad, gate_grad, xt, g, da, db, hgt = outs

    grad_gate, grad_up, grad_down, act_grad, gate_grad = weight_grads(
        xt, da.reshape(-1, hid), db.reshape(-1, hid), hgt, g.reshape(-1, width), act_grad, gate_grad)
    return act_grad, gate_grad.swapaxes(2, 3), grad_gate, grad_up, grad_down


def from_behind(value, axis, steps):
    count = lax.axis_size(axis)
    leading, last = (max(0, -steps), min(count, count - steps))
    return lax.ppermute(value, axis, [(source, source + steps) for source in range(leading, last)])


def silu_parts(pre_gate):
    sigmoid = jax.nn.sigmoid(pre_gate)
    return (pre_gate * sigmoid, sigmoid * (1.0 + pre_gate * (1.0 - sigmoid)))


def local(acts, out_grad, expert_ids, gates, w_gate, w_up, w_down):
    segments = lax.axis_size("segment")
    segment_now = lax.axis_index("segment")
    n_expert = lax.axis_size("expert")
    n_fsdp = lax.axis_size("fsdp")
    micro_count = acts.shape[1]
    tok_count = acts.shape[2]
    width = acts.shape[3]
    top_count = expert_ids.shape[3]
    capacity = 5 * top_count * tok_count // (4 * n_expert)
    w_first = w_gate[0, 0]
    w_third = w_up[0, 0]
    w_second = w_down[0, 0]
    hid_local = w_first.shape[1]
    expert_iota = jnp.arange(n_expert, dtype=jnp.int32)
    slot_iota = jnp.arange(capacity, dtype=jnp.int32)
    micro_iota = jnp.arange(micro_count, dtype=jnp.int32)
    contract_rows = (((0,), (0,)), ((), ()))
    contract_cols = (((1,), (1,)), ((), ()))
    grad_first = jnp.zeros((width, hid_local), jnp.float32)
    grad_third = jnp.zeros((width, hid_local), jnp.float32)
    grad_second = jnp.zeros((hid_local, width), jnp.float32)
    act_out = jnp.zeros(acts.shape, jnp.bfloat16)
    gate_out = jnp.zeros(gates.shape, jnp.float32)
    previous = jnp.zeros((tok_count, width), jnp.bfloat16)
    for moment in range(micro_count + segments - 1):
        micro_index = moment - (segments - 1 - segment_now)
        valid = (micro_index >= 0) & (micro_index < micro_count)
        picked = jnp.clip(micro_index, 0, micro_count - 1)
        tokens_now = lax.dynamic_index_in_dim(acts[0], picked, 0, keepdims=False)
        loss_grad = lax.dynamic_index_in_dim(out_grad, picked, 0, keepdims=False)
        ids_now = lax.dynamic_index_in_dim(expert_ids[0], picked, 0, keepdims=False)
        gates_now = lax.dynamic_index_in_dim(gates[0], picked, 0, keepdims=False)
        if moment > 0:
            incoming = from_behind(previous, "segment", -1)
        else:
            incoming = previous
        grad_now = jnp.where(segment_now == segments - 1, loss_grad, incoming)
        table = (ids_now[:, :, None] == expert_iota).astype(jnp.int32)
        counts = jnp.sum(table, axis=1)
        before = jnp.cumsum(counts, axis=0) - counts
        slots = jnp.sum(before[:, None, :] * table, axis=2)
        routing = (
            (ids_now[None, None] == expert_iota[:, None, None, None])
            & (slots[None, None] == slot_iota[None, :, None, None])
        ).astype(jnp.float32)
        placing = jnp.sum(routing, axis=3).astype(jnp.bfloat16)
        token_buf = jnp.einsum(
            "ect,td->ecd", placing, tokens_now, preferred_element_type=jnp.float32
        ).astype(jnp.bfloat16)
        grad_buf = jnp.einsum(
            "ect,td->ecd", placing, grad_now, preferred_element_type=jnp.float32
        ).astype(jnp.bfloat16)
        gate_buf = jnp.einsum("ectk,tk->ec", routing, gates_now.astype(jnp.float32)).astype(
            jnp.bfloat16
        )
        start_state = (
            grad_first,
            grad_third,
            grad_second,
            jnp.zeros((n_fsdp, n_expert, capacity, width), jnp.bfloat16),
            jnp.zeros((n_fsdp, n_expert, capacity), jnp.bfloat16),
        )
        grouped = (
            lax.all_gather(token_buf[None], "fsdp", axis=0, tiled=True),
            lax.all_gather(grad_buf[None], "fsdp", axis=0, tiled=True),
            lax.all_gather(gate_buf[None], "fsdp", axis=0, tiled=True),
        )
        token_rows = lax.all_to_all(grouped[0], "expert", split_axis=1, concat_axis=1, tiled=True)
        grad_rows = lax.all_to_all(grouped[1], "expert", split_axis=1, concat_axis=1, tiled=True)
        gate_rows = lax.all_to_all(grouped[2], "expert", split_axis=1, concat_axis=1, tiled=True)

        def compute(state):
            sum_first, sum_third, sum_second, part_rows, part_gates = state
            flat_tokens = token_rows.reshape(-1, width)
            flat_grads = grad_rows.reshape(-1, width)
            gate_col = gate_rows.reshape(-1).astype(jnp.float32)[:, None]
            pre_gate = jnp.dot(flat_tokens, w_first, preferred_element_type=jnp.float32)
            pre_up = jnp.dot(flat_tokens, w_third, preferred_element_type=jnp.float32)
            activated, slope_term = silu_parts(pre_gate)
            hidden = activated * pre_up
            back_hidden = lax.dot_general(
                flat_grads, w_second, contract_cols, preferred_element_type=jnp.float32
            )
            scaled = back_hidden * gate_col
            grad_gate_pre = (scaled * pre_up * slope_term).astype(jnp.bfloat16)
            grad_up_pre = (scaled * activated).astype(jnp.bfloat16)
            hidden_gated = (hidden * gate_col).astype(jnp.bfloat16)
            sum_first = sum_first + lax.dot_general(
                flat_tokens, grad_gate_pre, contract_rows, preferred_element_type=jnp.float32
            )
            sum_third = sum_third + lax.dot_general(
                flat_tokens, grad_up_pre, contract_rows, preferred_element_type=jnp.float32
            )
            sum_second = sum_second + lax.dot_general(
                hidden_gated, flat_grads, contract_rows, preferred_element_type=jnp.float32
            )
            partial_value = lax.dot_general(
                grad_gate_pre, w_first, contract_cols, preferred_element_type=jnp.float32
            )
            partial_value = partial_value + lax.dot_general(
                grad_up_pre, w_third, contract_cols, preferred_element_type=jnp.float32
            )
            gate_part = jnp.sum(hidden * back_hidden, axis=1)
            part_rows = partial_value.astype(jnp.bfloat16).reshape(token_rows.shape)
            part_gates = gate_part.astype(jnp.bfloat16).reshape(gate_rows.shape)
            return (sum_first, sum_third, sum_second, part_rows, part_gates)

        finished = lax.cond(valid, compute, lambda state: state, start_state)
        grad_first, grad_third, grad_second, part_rows, part_gates = finished
        summed_rows, summed_gates = (
            lax.psum_scatter(part_rows, "fsdp", scatter_dimension=0, tiled=True).astype(
                jnp.float32
            ),
            lax.psum_scatter(part_gates, "fsdp", scatter_dimension=0, tiled=True).astype(
                jnp.float32
            ),
        )
        back_rows, back_gates = (
            lax.all_to_all(
                summed_rows[0].astype(jnp.bfloat16),
                "expert",
                split_axis=0,
                concat_axis=0,
                tiled=True,
            ),
            lax.all_to_all(
                summed_gates[0].astype(jnp.bfloat16),
                "expert",
                split_axis=0,
                concat_axis=0,
                tiled=True,
            ),
        )
        token_back = jnp.einsum(
            "ect,ecd->td", placing, back_rows, preferred_element_type=jnp.float32
        )
        new_grad = (grad_now.astype(jnp.float32) + token_back).astype(jnp.bfloat16)
        gate_new = jnp.einsum("ectk,ec->tk", routing, back_gates.astype(jnp.float32))
        chosen = micro_iota == micro_index
        act_out = jnp.where(chosen[None, :, None, None], new_grad[None, None], act_out)
        gate_out = jnp.where(chosen[None, :, None, None], gate_new[None, None], gate_out)
        previous = new_grad
    return (
        act_out,
        gate_out,
        grad_first.astype(jnp.bfloat16)[None, None],
        grad_third.astype(jnp.bfloat16)[None, None],
        grad_second.astype(jnp.bfloat16)[None, None],
    )


def solution(mesh):
    in_specs = (
        P("segment", None, ("expert", "fsdp"), None),
        P(None, ("expert", "fsdp"), None),
        P("segment", None, ("expert", "fsdp"), None),
        P("segment", None, ("expert", "fsdp"), None),
        P("segment", "expert", None, "fsdp"),
        P("segment", "expert", None, "fsdp"),
        P("segment", "expert", "fsdp", None),
    )
    out_specs = (
        P("segment", None, ("expert", "fsdp"), None),
        P("segment", None, ("expert", "fsdp"), None),
        P("segment", "expert", None, "fsdp"),
        P("segment", "expert", None, "fsdp"),
        P("segment", "expert", "fsdp", None),
    )
    return jax.shard_map(relay, mesh=mesh, in_specs=in_specs, out_specs=out_specs, check_vma=False)
```

```python
import functools

import jax
import jax.numpy as jnp
from jax import lax
from jax.experimental import pallas as pl
from jax.experimental.pallas import tpu as pltpu
from jax.sharding import PartitionSpec as P

MESH = pl.DeviceIdType.MESH
LANES = 128
ROWS = 16
TILE = 256
GRANT = 62 << 20
ROOM = 44 << 20
PARTS = 1
CONTRACT_COLS = (((1,), (1,)), ((), ()))


def relay_kernel(
    segments, n_expert, n_fsdp,
    acts, out_grad, ids, gates, w_gate, w_up, w_down,
    act_out, gate_out, xt_out, g_out, da_out, db_out, hgt_out,
    wg, wu, wd, xbuf, gbuf, rbuf, zbuf, rst, zst, newg,
    slope_buf, act_buf, hid_buf, qbuf, da, db, hg, xt, hgt, wgt, wut, wdt,
    in_sem, out_sem, go, xs, xr, os, gr, ds, rs, rr, zs, zr,
):
    group = n_expert * n_fsdp
    micros, toks, width = acts.shape[1:]
    hid = wg.shape[1]
    rows = group * toks
    last = segments - 1
    part_width = newg.shape[2]
    parts = width // part_width
    seg = lax.axis_index("segment")
    expert = lax.axis_index("expert")
    fsdp = lax.axis_index("fsdp")
    me = expert * n_fsdp + fsdp
    is_last = seg == last
    tiles = [(s, min(TILE, hid - s)) for s in range(0, hid, TILE)]
    d_tiles = [(s, min(TILE, part_width - s)) for s in range(0, part_width, TILE)]

    def at(layer, member):
        return (layer, member // n_fsdp, member % n_fsdp)

    def turn_round(first, count, start, fn):
        def body(i, carry):
            fn((start + i) % count)
            return carry
        lax.fori_loop(first, count, body, 0)

    def others(fn):
        turn_round(1, group, me, fn)

    def members(fn):
        turn_round(0, group, me, fn)

    def other_experts(fn):
        turn_round(1, n_expert, expert, fn)

    def other_fsdp(fn):
        turn_round(1, n_fsdp, fsdp, fn)

    def own_loss(m, c):
        return pltpu.make_async_copy(
            out_grad.at[m, :, pl.ds(c * part_width, part_width)], gbuf.at[m * parts + c, me],
            in_sem.at[3 + micros + m * parts + c])

    own_acts = [
        pltpu.make_async_copy(acts.at[0, m], xbuf.at[m, me, :, pl.ds(0, width)], in_sem.at[3 + m])
        for m in range(micros)
    ]
    for copy in own_acts:
        copy.start()

    @pl.when(is_last)
    def _():
        for m in range(micros):
            for c in range(parts):
                own_loss(m, c).start()

    loads = [
        pltpu.make_async_copy(src.at[0, 0], dst, in_sem.at[i])
        for i, (src, dst) in enumerate(((w_gate, wg), (w_up, wu), (w_down, wd)))
    ]
    for load in loads:
        load.start()

    barrier = pltpu.get_barrier_semaphore()

    def greet(layer):
        def tell(j):
            pl.semaphore_signal(barrier, inc=1, device_id=at(layer, j), device_id_type=MESH)
        return tell

    others(greet(seg))

    @pl.when(seg > 0)
    def _():
        members(greet(seg - 1))

    @pl.when(seg < last)
    def _():
        members(greet(seg + 1))

    lane = lax.broadcasted_iota(jnp.int32, (toks, LANES), 1)
    for m in range(micros):
        named = ids[0, m].T
        weight = gates[0, m].astype(jnp.float32).T
        spread = jnp.zeros((toks, LANES), jnp.float32)
        for k in range(named.shape[1]):
            spread = spread + jnp.where(named[:, k : k + 1] == lane, weight[:, k : k + 1], 0.0)
        xbuf[m, me, :, width:] = spread.astype(jnp.bfloat16)

    below, above = (seg + last) // segments, (2 * last - seg) // segments
    pl.semaphore_wait(barrier, group - 1 + group * below + group * above)

    def x_copy(p, block, j, slot):
        return pltpu.make_async_remote_copy(
            xbuf.at[p, block], xbuf.at[p, block], xs.at[p, slot], xr.at[p, block],
            device_id=at(seg, j), device_id_type=MESH)

    def own_copy(p, block, j, slot):
        return pltpu.make_async_remote_copy(
            gbuf.at[p, block], gbuf.at[p, block], os.at[p, slot], gr.at[p, block],
            device_id=at(seg, j), device_id_type=MESH)

    def down_copy(p, block, j):
        return pltpu.make_async_remote_copy(
            newg.at[p], gbuf.at[p, block], ds.at[p, j], gr.at[p, block],
            device_id=at(lax.max(seg - 1, 0), j), device_id_type=MESH)

    def r_copy(p, block, j):
        return pltpu.make_async_remote_copy(
            rst.at[p, j], rbuf.at[p, block], rs.at[p, j], rr.at[p, block],
            device_id=at(seg, j), device_id_type=MESH)

    def z_copy(block, j):
        return pltpu.make_async_remote_copy(
            zst.at[j], zbuf.at[block], zs.at[j], zr.at[block],
            device_id=at(seg, j), device_id_type=MESH)

    def spread_own(copy, p):
        def along(e):
            j = e * n_fsdp + fsdp
            copy(p, me, j, j).start()

        def across(f):
            j = expert * n_fsdp + f
            copy(p, me, j, j).start()

        other_experts(along)
        other_fsdp(across)

    def pass_on(copy, p):
        def along(e):
            block = e * n_fsdp + fsdp
            copy(p, block, block, block).wait_recv()

            def across(f):
                copy(p, block, expert * n_fsdp + f, e * n_fsdp + f).start()

            other_fsdp(across)

        other_experts(along)

    def take_rest(copy, p):
        def across(f):
            def along(e, carry):
                block = e * n_fsdp + f
                copy(p, block, block, block).wait_recv()
                return carry
            lax.fori_loop(0, n_expert, along, 0)
        other_fsdp(across)

    def spread_sent(copy, p):
        others(lambda j: copy(p, me, j, j).wait_send())

    def pieces(m):
        return range(m * parts, (m + 1) * parts)

    def send_loss(m):
        for c in range(parts):
            own_loss(m, c).wait()
        for p in pieces(m):
            spread_own(own_copy, p)

    def pass_loss(m):
        for p in pieces(m):
            pass_on(own_copy, p)

    def allow_next():
        @pl.when(seg > 0)
        def _():
            pl.semaphore_signal(go, inc=1, device_id=at(seg - 1, me), device_id_type=MESH)

    for copy in own_acts:
        copy.wait()

    @pl.when(is_last)
    def _():
        for m in range(micros):
            spread_own(x_copy, m)
            send_loss(m)
        pass_on(x_copy, 0)
        pass_loss(0)
        take_rest(x_copy, 0)
        allow_next()

    for load in loads:
        load.wait()

    @pl.when(seg < last)
    def _():
        for src, dst in ((wg, wgt), (wu, wut), (wd, wdt)):
            for s in range(0, src.shape[0], TILE):
                e = min(s + TILE, src.shape[0])
                dst[:, s:e] = src[s:e, :].T
        pl.semaphore_wait(go, 1)
        for m in range(micros):
            spread_own(x_copy, m)
        for m in range(micros):
            pass_on(x_copy, m)
        for m in range(micros):
            take_rest(x_copy, m)
        allow_next()

    stores = []

    def keep(src, dst):
        copy = pltpu.make_async_copy(src, dst, out_sem.at[len(stores)])
        copy.start()
        stores.append(copy)

    def prepare(m):
        x = xbuf[m, :, :, :width].reshape(rows, width)
        weights = xbuf[m, :, :, width:].reshape(rows, LANES).astype(jnp.float32)
        mine = lax.broadcasted_iota(jnp.int32, (rows, LANES), 1) == expert
        c = jnp.sum(jnp.where(mine, weights, 0.0), axis=1, keepdims=True)
        for s, size in tiles:
            cut = slice(s, s + size)
            a = jnp.dot(x, wg[:, cut], preferred_element_type=jnp.float32)
            b = jnp.dot(x, wu[:, cut], preferred_element_type=jnp.float32)
            sigmoid = jax.nn.sigmoid(a)
            silu = a * sigmoid
            hidden = silu * b
            slope_buf[m, :, cut] = c * b * (sigmoid * (1.0 + a * (1.0 - sigmoid)))
            act_buf[m, :, cut] = c * silu
            hid_buf[m, :, cut] = hidden
            hg[m, :, cut] = (hidden * c).astype(jnp.bfloat16)

    def transpose(m):
        cut = slice(m * rows, (m + 1) * rows)
        xt[:, cut] = xbuf[m, :, :, :width].reshape(rows, width).T
        hgt[:, cut] = hg[m].T

    def times(left, kept, turned, cut, along, flat):
        if flat:
            return lax.dot_general(
                left, kept[cut, along], CONTRACT_COLS, preferred_element_type=jnp.float32)
        return jnp.dot(left, turned[along, cut], preferred_element_type=jnp.float32)

    def partial(m, flat):
        z = jnp.zeros((rows, 1), jnp.float32)
        for c, p in enumerate(pieces(m)):
            if flat:
                take_rest(own_copy, p)
            else:
                members(lambda j: own_copy(p, j, j, j).wait_recv())

            g = gbuf[p].reshape(rows, part_width)
            columns = slice(c * part_width, (c + 1) * part_width)
            for s, size in tiles:
                cut = slice(s, s + size)
                q = times(g, wd, wdt, cut, columns, flat)
                if c > 0:
                    q = q + qbuf[:, cut]
                if c < parts - 1:
                    qbuf[:, cut] = q
                else:
                    da[m, :, cut] = (q * slope_buf[m, :, cut]).astype(jnp.bfloat16)
                    db[m, :, cut] = (q * act_buf[m, :, cut]).astype(jnp.bfloat16)
                    z = z + jnp.sum(q * hid_buf[m, :, cut], axis=1, keepdims=True)
        for c, p in enumerate(pieces(m)):
            for s, size in d_tiles:
                cut = slice(c * part_width + s, c * part_width + s + size)
                r = times(da[m], wg, wgt, cut, slice(None), flat)
                r = r + times(db[m], wu, wut, cut, slice(None), flat)
                rst[p, :, :, s : s + size] = r.astype(jnp.bfloat16).reshape(group, toks, size)
            others(lambda j: r_copy(p, me, j).start())
            rbuf[p, me] = rst[p, me]
        zst[:, m] = jnp.broadcast_to(z, (rows, LANES)).astype(jnp.bfloat16).reshape(group, toks, LANES)

    def combine(m):
        for c, p in enumerate(pieces(m)):
            others(lambda j: r_copy(p, j, j).wait_recv())
            total = gbuf[p, me].astype(jnp.float32)
            for e in range(n_expert):
                part = rbuf[p, e * n_fsdp].astype(jnp.float32)
                for f in range(1, n_fsdp):
                    part = part + rbuf[p, e * n_fsdp + f].astype(jnp.float32)
                total = total + part.astype(jnp.bfloat16).astype(jnp.float32)
            fresh = total.astype(jnp.bfloat16)
            newg[p] = fresh

            @pl.when(seg > 0)
            def _():
                members(lambda j: down_copy(p, me, j).start())

            act_out[0, m, :, c * part_width : (c + 1) * part_width] = fresh

    prepare(0)

    @pl.when(is_last)
    def _():
        for m in range(1, micros):
            pass_on(x_copy, m)
            pass_loss(m)

    @pl.when(seg < last)
    def _():
        for m in range(1, micros):
            prepare(m)

    @pl.when(seg == 0)
    def _():
        for m in range(micros):
            if segments > 1:
                transpose(m)

    for m in range(micros):
        if m > 0:
            @pl.when(is_last)
            def _():
                take_rest(x_copy, m)
                prepare(m)

        @pl.when(is_last)
        def _():
            partial(m, True)

        if segments > 1:
            @pl.when(seg < last)
            def _():
                partial(m, False)

    zbuf[me] = zst[me]
    others(lambda j: z_copy(me, j).start())
    for m in range(micros):
        for c, p in enumerate(pieces(m)):
            keep(gbuf.at[p], g_out.at[m, :, :, pl.ds(c * part_width, part_width)])
        keep(da.at[m], da_out.at[m])
        keep(db.at[m], db_out.at[m])
    turned = [
        pltpu.make_async_copy(src, dst, out_sem.at[len(stores) + i])
        for i, (src, dst) in enumerate(((xt, xt_out), (hgt, hgt_out)))
    ]
    early = seg + (segments == 1) == 0
    late = seg + (segments == 1) > 0

    @pl.when(early)
    def _():
        for copy in turned:
            copy.start()

    for m in range(micros):
        combine(m)

    @pl.when(late)
    def _():
        for m in range(micros):
            transpose(m)
        for copy in turned:
            copy.start()

    others(lambda j: z_copy(j, j).wait_recv())
    for m in range(micros):
        named = ids[0, m].T
        total = jnp.zeros(named.shape, jnp.float32)
        for e in range(n_expert):
            part = zbuf[e * n_fsdp, m].astype(jnp.float32)
            for f in range(1, n_fsdp):
                part = part + zbuf[e * n_fsdp + f, m].astype(jnp.float32)
            part = part.astype(jnp.bfloat16).astype(jnp.float32)
            total = total + jnp.where(named == e, part[:, : named.shape[1]], 0.0)
        gate_out[0, m] = total.T

    for m in range(micros):
        spread_sent(x_copy, m)
        for p in pieces(m):
            others(lambda j: r_copy(p, me, j).wait_send())

            @pl.when(is_last)
            def _():
                spread_sent(own_copy, p)

            @pl.when(seg > 0)
            def _():
                members(lambda j: down_copy(p, me, j).wait_send())
    others(lambda j: z_copy(me, j).wait_send())
    for copy in stores + turned:
        copy.wait()


def weight_kernel(
    xt, da, db, hgt, g, act, gate, grad_gate, grad_up, grad_down, act_out, gate_out,
    xt_v, da_v, db_v, hgt_v, g_v, made, in_sem, out_sem,
):
    loads = [
        pltpu.make_async_copy(src, dst, in_sem.at[i])
        for i, (src, dst) in enumerate(((xt, xt_v), (da, da_v), (db, db_v), (hgt, hgt_v), (g, g_v)))
    ]
    for load in loads:
        load.start()
    stores = [
        pltpu.make_async_copy(src, dst, out_sem.at[i])
        for i, (src, dst) in enumerate(((act, act_out), (gate, gate_out)))
    ]
    for copy in stores:
        copy.start()
    products = (
        (xt_v, da_v, grad_gate, loads[:2]),
        (xt_v, db_v, grad_up, loads[2:3]),
        (hgt_v, g_v, grad_down, loads[3:]),
    )
    base = 0
    for left, right, result, needed in products:
        for load in needed:
            load.wait()
        height, columns = left.shape[0], right.shape[1]
        for s in range(0, height, TILE):
            size = min(TILE, height - s)
            tile = jnp.dot(left[s : s + size, :], right[...], preferred_element_type=jnp.float32)
            place = made.at[pl.ds(base + s, size), pl.ds(0, columns)]
            place[...] = tile.astype(jnp.bfloat16)
            copy = pltpu.make_async_copy(
                place, result.at[0, 0, pl.ds(s, size)], out_sem.at[len(stores)])
            copy.start()
            stores.append(copy)
        base += height
    for copy in stores:
        copy.wait()


def weight_grads(xt, da, db, hgt, g, act, gate):
    width, rows = xt.shape
    hid = da.shape[1]
    bf16 = jnp.bfloat16
    far = pl.BlockSpec(memory_space=pl.ANY)
    stores = 2 + 2 * -(-width // TILE) + -(-hid // TILE)
    return pl.pallas_call(
        weight_kernel,
        out_shape=(
            jax.ShapeDtypeStruct((1, 1, width, hid), bf16),
            jax.ShapeDtypeStruct((1, 1, width, hid), bf16),
            jax.ShapeDtypeStruct((1, 1, hid, width), bf16),
            jax.ShapeDtypeStruct(act.shape, act.dtype),
            jax.ShapeDtypeStruct(gate.shape, gate.dtype),
        ),
        in_specs=[far] * 7,
        out_specs=(far,) * 5,
        scratch_shapes=[
            pltpu.VMEM((width, rows), bf16),
            pltpu.VMEM((rows, hid), bf16),
            pltpu.VMEM((rows, hid), bf16),
            pltpu.VMEM((hid, rows), bf16),
            pltpu.VMEM((rows, width), bf16),
            pltpu.VMEM((2 * width + hid, max(width, hid)), bf16),
            pltpu.SemaphoreType.DMA((5,)),
            pltpu.SemaphoreType.DMA((stores,)),
        ],
        compiler_params=pltpu.CompilerParams(vmem_limit_bytes=GRANT),
        cost_estimate=pl.CostEstimate(
            flops=6 * rows * width * hid, bytes_accessed=6 * width * hid, transcendentals=0
        ),
    )(xt, da, db, hgt, g, act, gate)


def relay_room(acts, w_gate, group):
    micros, toks, width = acts.shape[1:]
    hid = w_gate.shape[3]
    rows = micros * group * toks
    return 6 * width * hid * 2 + rows * (width * 2 * 4 + hid * (4 * 4 + 4 * 2) + width * 2 + LANES * 6)


def relay(acts, out_grad, ids, gates, w_gate, w_up, w_down):
    segments = lax.axis_size("segment")
    n_expert = lax.axis_size("expert")
    n_fsdp = lax.axis_size("fsdp")
    group = n_expert * n_fsdp
    micros, toks, width = acts.shape[1:]
    hid = w_gate.shape[3]
    fits = (
        toks % ROWS == 0
        and group * toks % LANES == 0
        and width % LANES == 0
        and hid % LANES == 0
        and n_expert <= LANES
        and relay_room(acts, w_gate, group) <= ROOM
    )
    if not fits:
        return local(acts, out_grad, ids, gates, w_gate, w_up, w_down)
    rows = group * toks
    parts = PARTS if width % (PARTS * LANES) == 0 else 1
    pieces = micros * parts
    piece = (pieces, group, toks, width // parts)
    bf16, f32 = jnp.bfloat16, jnp.float32
    vmem = pl.BlockSpec(memory_space=pltpu.VMEM)
    far = pl.BlockSpec(memory_space=pl.ANY)
    home = pl.BlockSpec(memory_space=pltpu.HBM)
    dma = pltpu.SemaphoreType.DMA
    scratch = [
        pltpu.VMEM((width, hid), bf16),
        pltpu.VMEM((width, hid), bf16),
        pltpu.VMEM((hid, width), bf16),
        pltpu.VMEM((micros, group, toks, width + LANES), bf16),
        pltpu.VMEM(piece, bf16),
        pltpu.VMEM(piece, bf16),
        pltpu.VMEM((group, micros, toks, LANES), bf16),
        pltpu.VMEM(piece, bf16),
        pltpu.VMEM((group, micros, toks, LANES), bf16),
        pltpu.VMEM((pieces, toks, width // parts), bf16),
    ]
    scratch += [pltpu.VMEM((micros, rows, hid), f32)] * 3
    scratch += [pltpu.VMEM((rows, hid), f32)]
    scratch += [pltpu.VMEM((micros, rows, hid), bf16)] * 3
    scratch += [pltpu.VMEM((width, micros * rows), bf16), pltpu.VMEM((hid, micros * rows), bf16)]
    scratch += [pltpu.VMEM((hid, width), bf16)] * 2 + [pltpu.VMEM((width, hid), bf16)]
    scratch += [dma((3 + micros + pieces,)), dma((2 + 2 * micros + pieces,))]
    scratch += [pltpu.SemaphoreType.REGULAR]
    scratch += [dma((micros, group))] * 2
    scratch += [dma((pieces, group))] * 5
    scratch += [dma((group,))] * 2
    flops = 2 * micros * rows * width * hid * 5
    outs = pl.pallas_call(
        functools.partial(relay_kernel, segments, n_expert, n_fsdp),
        out_shape=(
            jax.ShapeDtypeStruct(acts.shape, bf16),
            jax.ShapeDtypeStruct(gates.shape[:2] + (gates.shape[3], toks), f32),
            jax.ShapeDtypeStruct((width, micros * rows), bf16),
            jax.ShapeDtypeStruct((micros, group, toks, width), bf16),
            jax.ShapeDtypeStruct((micros, rows, hid), bf16),
            jax.ShapeDtypeStruct((micros, rows, hid), bf16),
            jax.ShapeDtypeStruct((hid, micros * rows), bf16),
        ),
        in_specs=[home, home, vmem, vmem, far, far, far],
        out_specs=(vmem, vmem, far, far, far, far, far),
        scratch_shapes=scratch,
        compiler_params=pltpu.CompilerParams(
            collective_id=0, has_side_effects=True, vmem_limit_bytes=GRANT
        ),
        cost_estimate=pl.CostEstimate(
            flops=flops, bytes_accessed=6 * width * hid, transcendentals=micros * rows * hid
        ),
    )(acts, out_grad, ids.swapaxes(2, 3), gates.swapaxes(2, 3), w_gate, w_up, w_down)
    act_grad, gate_grad, xt, g, da, db, hgt = outs

    grad_gate, grad_up, grad_down, act_grad, gate_grad = weight_grads(
        xt, da.reshape(-1, hid), db.reshape(-1, hid), hgt, g.reshape(-1, width), act_grad, gate_grad)
    return act_grad, gate_grad.swapaxes(2, 3), grad_gate, grad_up, grad_down


def from_behind(value, axis, steps):
    count = lax.axis_size(axis)
    leading, last = (max(0, -steps), min(count, count - steps))
    return lax.ppermute(value, axis, [(source, source + steps) for source in range(leading, last)])


def silu_parts(pre_gate):
    sigmoid = jax.nn.sigmoid(pre_gate)
    return (pre_gate * sigmoid, sigmoid * (1.0 + pre_gate * (1.0 - sigmoid)))


def local(acts, out_grad, expert_ids, gates, w_gate, w_up, w_down):
    segments = lax.axis_size("segment")
    segment_now = lax.axis_index("segment")
    n_expert = lax.axis_size("expert")
    n_fsdp = lax.axis_size("fsdp")
    micro_count = acts.shape[1]
    tok_count = acts.shape[2]
    width = acts.shape[3]
    top_count = expert_ids.shape[3]
    capacity = 5 * top_count * tok_count // (4 * n_expert)
    w_first = w_gate[0, 0]
    w_third = w_up[0, 0]
    w_second = w_down[0, 0]
    hid_local = w_first.shape[1]
    expert_iota = jnp.arange(n_expert, dtype=jnp.int32)
    slot_iota = jnp.arange(capacity, dtype=jnp.int32)
    micro_iota = jnp.arange(micro_count, dtype=jnp.int32)
    contract_rows = (((0,), (0,)), ((), ()))
    contract_cols = (((1,), (1,)), ((), ()))
    grad_first = jnp.zeros((width, hid_local), jnp.float32)
    grad_third = jnp.zeros((width, hid_local), jnp.float32)
    grad_second = jnp.zeros((hid_local, width), jnp.float32)
    act_out = jnp.zeros(acts.shape, jnp.bfloat16)
    gate_out = jnp.zeros(gates.shape, jnp.float32)
    previous = jnp.zeros((tok_count, width), jnp.bfloat16)
    for moment in range(micro_count + segments - 1):
        micro_index = moment - (segments - 1 - segment_now)
        valid = (micro_index >= 0) & (micro_index < micro_count)
        picked = jnp.clip(micro_index, 0, micro_count - 1)
        tokens_now = lax.dynamic_index_in_dim(acts[0], picked, 0, keepdims=False)
        loss_grad = lax.dynamic_index_in_dim(out_grad, picked, 0, keepdims=False)
        ids_now = lax.dynamic_index_in_dim(expert_ids[0], picked, 0, keepdims=False)
        gates_now = lax.dynamic_index_in_dim(gates[0], picked, 0, keepdims=False)
        if moment > 0:
            incoming = from_behind(previous, "segment", -1)
        else:
            incoming = previous
        grad_now = jnp.where(segment_now == segments - 1, loss_grad, incoming)
        table = (ids_now[:, :, None] == expert_iota).astype(jnp.int32)
        counts = jnp.sum(table, axis=1)
        before = jnp.cumsum(counts, axis=0) - counts
        slots = jnp.sum(before[:, None, :] * table, axis=2)
        routing = (
            (ids_now[None, None] == expert_iota[:, None, None, None])
            & (slots[None, None] == slot_iota[None, :, None, None])
        ).astype(jnp.float32)
        placing = jnp.sum(routing, axis=3).astype(jnp.bfloat16)
        token_buf = jnp.einsum(
            "ect,td->ecd", placing, tokens_now, preferred_element_type=jnp.float32
        ).astype(jnp.bfloat16)
        grad_buf = jnp.einsum(
            "ect,td->ecd", placing, grad_now, preferred_element_type=jnp.float32
        ).astype(jnp.bfloat16)
        gate_buf = jnp.einsum("ectk,tk->ec", routing, gates_now.astype(jnp.float32)).astype(
            jnp.bfloat16
        )
        start_state = (
            grad_first,
            grad_third,
            grad_second,
            jnp.zeros((n_fsdp, n_expert, capacity, width), jnp.bfloat16),
            jnp.zeros((n_fsdp, n_expert, capacity), jnp.bfloat16),
        )
        grouped = (
            lax.all_gather(token_buf[None], "fsdp", axis=0, tiled=True),
            lax.all_gather(grad_buf[None], "fsdp", axis=0, tiled=True),
            lax.all_gather(gate_buf[None], "fsdp", axis=0, tiled=True),
        )
        token_rows = lax.all_to_all(grouped[0], "expert", split_axis=1, concat_axis=1, tiled=True)
        grad_rows = lax.all_to_all(grouped[1], "expert", split_axis=1, concat_axis=1, tiled=True)
        gate_rows = lax.all_to_all(grouped[2], "expert", split_axis=1, concat_axis=1, tiled=True)

        def compute(state):
            sum_first, sum_third, sum_second, part_rows, part_gates = state
            flat_tokens = token_rows.reshape(-1, width)
            flat_grads = grad_rows.reshape(-1, width)
            gate_col = gate_rows.reshape(-1).astype(jnp.float32)[:, None]
            pre_gate = jnp.dot(flat_tokens, w_first, preferred_element_type=jnp.float32)
            pre_up = jnp.dot(flat_tokens, w_third, preferred_element_type=jnp.float32)
            activated, slope_term = silu_parts(pre_gate)
            hidden = activated * pre_up
            back_hidden = lax.dot_general(
                flat_grads, w_second, contract_cols, preferred_element_type=jnp.float32
            )
            scaled = back_hidden * gate_col
            grad_gate_pre = (scaled * pre_up * slope_term).astype(jnp.bfloat16)
            grad_up_pre = (scaled * activated).astype(jnp.bfloat16)
            hidden_gated = (hidden * gate_col).astype(jnp.bfloat16)
            sum_first = sum_first + lax.dot_general(
                flat_tokens, grad_gate_pre, contract_rows, preferred_element_type=jnp.float32
            )
            sum_third = sum_third + lax.dot_general(
                flat_tokens, grad_up_pre, contract_rows, preferred_element_type=jnp.float32
            )
            sum_second = sum_second + lax.dot_general(
                hidden_gated, flat_grads, contract_rows, preferred_element_type=jnp.float32
            )
            partial_value = lax.dot_general(
                grad_gate_pre, w_first, contract_cols, preferred_element_type=jnp.float32
            )
            partial_value = partial_value + lax.dot_general(
                grad_up_pre, w_third, contract_cols, preferred_element_type=jnp.float32
            )
            gate_part = jnp.sum(hidden * back_hidden, axis=1)
            part_rows = partial_value.astype(jnp.bfloat16).reshape(token_rows.shape)
            part_gates = gate_part.astype(jnp.bfloat16).reshape(gate_rows.shape)
            return (sum_first, sum_third, sum_second, part_rows, part_gates)

        finished = lax.cond(valid, compute, lambda state: state, start_state)
        grad_first, grad_third, grad_second, part_rows, part_gates = finished
        summed_rows, summed_gates = (
            lax.psum_scatter(part_rows, "fsdp", scatter_dimension=0, tiled=True).astype(
                jnp.float32
            ),
            lax.psum_scatter(part_gates, "fsdp", scatter_dimension=0, tiled=True).astype(
                jnp.float32
            ),
        )
        back_rows, back_gates = (
            lax.all_to_all(
                summed_rows[0].astype(jnp.bfloat16),
                "expert",
                split_axis=0,
                concat_axis=0,
                tiled=True,
            ),
            lax.all_to_all(
                summed_gates[0].astype(jnp.bfloat16),
                "expert",
                split_axis=0,
                concat_axis=0,
                tiled=True,
            ),
        )
        token_back = jnp.einsum(
            "ect,ecd->td", placing, back_rows, preferred_element_type=jnp.float32
        )
        new_grad = (grad_now.astype(jnp.float32) + token_back).astype(jnp.bfloat16)
        gate_new = jnp.einsum("ectk,ec->tk", routing, back_gates.astype(jnp.float32))
        chosen = micro_iota == micro_index
        act_out = jnp.where(chosen[None, :, None, None], new_grad[None, None], act_out)
        gate_out = jnp.where(chosen[None, :, None, None], gate_new[None, None], gate_out)
        previous = new_grad
    return (
        act_out,
        gate_out,
        grad_first.astype(jnp.bfloat16)[None, None],
        grad_third.astype(jnp.bfloat16)[None, None],
        grad_second.astype(jnp.bfloat16)[None, None],
    )


def solution(mesh):
    in_specs = (
        P("segment", None, ("expert", "fsdp"), None),
        P(None, ("expert", "fsdp"), None),
        P("segment", None, ("expert", "fsdp"), None),
        P("segment", None, ("expert", "fsdp"), None),
        P("segment", "expert", None, "fsdp"),
        P("segment", "expert", None, "fsdp"),
        P("segment", "expert", "fsdp", None),
    )
    out_specs = (
        P("segment", None, ("expert", "fsdp"), None),
        P("segment", None, ("expert", "fsdp"), None),
        P("segment", "expert", None, "fsdp"),
        P("segment", "expert", None, "fsdp"),
        P("segment", "expert", "fsdp", None),
    )
    return jax.shard_map(relay, mesh=mesh, in_specs=in_specs, out_specs=out_specs, check_vma=False)
```
